256 devices in a mesh: band: 4 (over z_lo), col: 64 (over z_hi, y, x, core).
Axes of the slice: x: 4, y: 4, z: 8 (z_hi: 2, z_lo: 4; z = z_hi * 4 + z_lo), core: 2. Of those that a mesh axis runs over, the one named last changes fastest.
Arguments:
- fields: bfloat16 [4, 80, 32, 8192], P(None, None, 'band', 'col'), may hold values from -6 to 6
- inverse: bfloat16 [4, 80, 80], replicated, may hold values from -1 to 2
- block_costs: int32 [64, 32], P('col', 'band'), may hold values from 1 to 8, as said below
- row_length: int32 [32], P('band'), may hold values from 4097 to 8192
Outputs:
- spectra: float32 [320, 32, 2, 2048], P('col', None, None, 'band')
The draws below stay inside these ranges and needn't reach their ends.
Inputs may be any that keep to these rules, and one draw needn't show every extreme that they name: `block_costs`: at least one block takes 8 substeps and at least one takes 1.
All inputs are finite; a program needn't handle non-finite values.
Results may differ from the reference program's by a relative error of at most 0.0042.
Values may be sent and summed in bfloat16 or wider, within the bound.
No kernel may reach another device: no remote copies, remote signals or barrier semaphores. Data moves between devices by JAX's collectives and lax.ppermute only.
A program may use at most 64 MiB of HBM per device.

```python
import math
import jax
import jax.numpy as jnp
from jax import lax

FIELDS = 4
LEV = 80
BLOCK = 128
CMAX = 8
ROWS = 32
NLON = 8192
WAVES = 2048
N_COL = 64


def draw_inverse(key, part):
    key_diag, key_off = jax.random.split(jax.random.fold_in(key, 11))
    diagonal_part = 0.5 + 0.4 * jax.random.uniform(key_diag, (FIELDS, LEV), jnp.float32)
    off_part = jnp.clip(jax.random.normal(key_off, (FIELDS, LEV, LEV), jnp.float32), -1.7, 1.7) * 0.35
    off_part = off_part / jnp.sqrt(jnp.float32(LEV))
    identity = jnp.eye(LEV, dtype=jnp.float32)
    return (off_part + diagonal_part[:, :, None] * identity[None, :, :]).astype(jnp.bfloat16)


def draw_block_costs(key, part):
    key_heavy, key_cost = jax.random.split(jax.random.fold_in(key, 23))
    heavy_mask = jax.random.randint(key_heavy, (N_COL, 1), 0, 4) == 0
    top_cost = jnp.where(heavy_mask, CMAX, 1).astype(jnp.int32)
    costs_drawn = 1 + jax.random.randint(key_cost, (N_COL, ROWS), 0, top_cost)
    costs_drawn = costs_drawn.at[0, 0].set(CMAX).at[0, 1].set(1)
    return costs_drawn.astype(jnp.int32)


def set_ends(drawn, own_key, low, top_value):
    place = [jax.random.randint(jax.random.fold_in(own_key, axis), (), 0, length) for axis, length in enumerate(drawn.shape)]
    main_axis = drawn.shape.index(max(drawn.shape))
    next_to = place[:main_axis] + [(place[main_axis] + 1) % drawn.shape[main_axis]] + place[main_axis + 1:]
    return drawn.at[tuple(place)].set(low).at[tuple(next_to)].set(top_value)


def block_scale(stream_key, extent, cuts, smallest, largest):
    loudness, own = 1.0, jax.random.fold_in(stream_key, 6)
    for axis_at, shards_of in cuts:
        steps = jnp.exp(jax.random.uniform(jax.random.fold_in(own, axis_at), (shards_of,), jnp.float32, smallest / len(cuts), largest / len(cuts)))
        loudness = loudness * jnp.repeat(steps, extent[axis_at] // shards_of).reshape([-1 if axis == axis_at else 1 for axis in range(len(extent))])
    return loudness


def bell_draw(own_key, shape, width, limit, cuts=(), kind=jnp.bfloat16):
    drawn = width * jax.random.normal(own_key, shape, jnp.float32)
    if cuts:
        drawn = drawn * block_scale(own_key, shape, cuts, -0.22, 0.18)
    return jnp.clip(drawn, -limit, limit).astype(kind)


def setup_inputs(seed: int = 0) -> dict:
    key_list = jax.random.split(jax.random.key(seed), 5)
    return {
        "fields": bell_draw(key_list[0], (FIELDS, LEV, ROWS, NLON), 1.0, 6.0, ((2, 4), (3, 64))),
        "inverse": draw_inverse(jax.random.fold_in(key_list[4], 71), 0),
        "block_costs": draw_block_costs(jax.random.fold_in(key_list[4], 71), 0),
        "row_length": set_ends(jax.random.randint(key_list[3], (ROWS,), NLON // 2 + 1, NLON + 1), jax.random.fold_in(key_list[3], 1), NLON // 2 + 1, NLON).astype(jnp.int32),
    }


def reference(fields, inverse, block_costs, row_length):
    inverse_f32 = inverse.astype(jnp.float32)

    def row_spectrum(operands):
        field_row, cost_row, length_row = operands
        initial = field_row.reshape(FIELDS, LEV, N_COL, BLOCK)
        relaxed = initial
        for sweep_index in range(CMAX):
            applied = jnp.einsum('fkl,flcb->fkcb', inverse_f32, relaxed.astype(jnp.float32), precision=lax.Precision.HIGHEST).astype(jnp.bfloat16)
            relaxed = jnp.where((sweep_index < cost_row)[None, None, :, None], applied, relaxed)
        tendency = (relaxed.astype(jnp.float32) - initial.astype(jnp.float32)).astype(jnp.bfloat16)
        tendency = lax.optimization_barrier(tendency)
        updated = (initial.astype(jnp.float32) + tendency.astype(jnp.float32)).astype(jnp.bfloat16)
        updated = updated.reshape(FIELDS * LEV, NLON)
        longitude = jnp.arange(NLON, dtype=jnp.int32)
        masked = jnp.where(longitude[None, :] < length_row, updated, jnp.zeros_like(updated))
        spectrum = jnp.fft.rfft(masked.astype(jnp.float32), axis=-1)[:, :WAVES]
        scale_factor = 1.0 / math.sqrt(NLON)
        parts = jnp.stack([jnp.real(spectrum), jnp.imag(spectrum)], axis=1).astype(jnp.float32)
        return parts * scale_factor
    per_row = lax.map(row_spectrum, (jnp.moveaxis(fields, 2, 0), block_costs.T, row_length))
    return jnp.transpose(per_row, (1, 0, 2, 3))
```

```python
import math

import jax
import jax.numpy as jnp
import numpy as np
from jax import lax
from jax.experimental import pallas as pl
from jax.experimental.pallas import tpu as pltpu
from jax.sharding import PartitionSpec as P

f32 = jnp.float32
bf16 = jnp.bfloat16
VMEM_BYTES = 40 * 1024 * 1024

FIELDS = 4
LEV = 80
ROWS = 8
BLOCK = 128
N_COL = 64
N_BAND = 4
NLON = N_COL * BLOCK
WAVES = 2048
TILES = WAVES // BLOCK
LEVELS = FIELDS * LEV // N_COL


def split_bf16(table):
    high = table.astype(np.float32).astype(jnp.bfloat16)
    low = (table - high.astype(np.float64)).astype(np.float32).astype(jnp.bfloat16)
    return high, low


def tables():
    q = np.arange(N_COL)
    angle = 2.0 * np.pi / N_COL * ((q[:, None] * q[None, :]) % N_COL)
    inner = np.concatenate([np.cos(angle), -np.sin(angle)], axis=0)
    inner = np.concatenate(split_bf16(inner), axis=1)
    u = np.arange(BLOCK)
    angle = 2.0 * np.pi / NLON * (u[:, None] * u[None, :])
    twiddle = np.stack([np.cos(angle), np.sin(angle)]).astype(np.float32)
    t = np.arange(TILES)
    angle = 2.0 * np.pi / (NLON // BLOCK) * ((t[:, None] * u[None, :]) % (NLON // BLOCK))
    cosine, sine = np.cos(angle), np.sin(angle)
    real_row = np.concatenate([cosine, sine], axis=1)
    imag_row = np.concatenate([-sine, cosine], axis=1)
    outer = np.stack([real_row, imag_row], axis=1).reshape(2 * TILES, 2 * BLOCK) / math.sqrt(NLON)
    outer = np.concatenate(split_bf16(outer), axis=0)
    return inner, twiddle, outer


def relax_kernel(cost_ref, length_ref, fields_ref, inverse_ref, out_ref, flat, state):
    first = lax.axis_index("col") * BLOCK
    flat[...] = fields_ref[...].astype(f32).reshape(FIELDS * LEV * ROWS, BLOCK)
    for f in range(FIELDS):
        for r in range(ROWS):
            piece = flat[pl.ds(f * LEV * ROWS + r, LEV, stride=ROWS), :]
            state[f, :, r * BLOCK:(r + 1) * BLOCK] = piece.astype(bf16)
    costs = [cost_ref[0, r] for r in range(ROWS)]
    most = costs[0]
    for r in range(1, ROWS):
        most = jnp.maximum(most, costs[r])
    cost_lanes = jnp.concatenate([jnp.full((1, BLOCK), costs[r], jnp.int32) for r in range(ROWS)], axis=1)

    @pl.loop(0, most)
    def _(s):
        active = s < cost_lanes
        for f in range(FIELDS):
            now = state[f]
            new = jnp.dot(inverse_ref[f], now, preferred_element_type=f32)
            state[f] = jnp.where(active, new, now.astype(f32)).astype(bf16)

    lane = first + lax.broadcasted_iota(jnp.int32, (1, BLOCK), 1)
    for r in range(ROWS):
        keep = lane < length_ref[r]
        for f in range(FIELDS):
            rows = pl.ds(f * LEV * ROWS + r, LEV, stride=ROWS)
            initial = flat[rows, :]
            relaxed = state[f, :, r * BLOCK:(r + 1) * BLOCK].astype(f32)
            tendency = (relaxed - initial).astype(bf16).astype(f32)
            updated = (initial + tendency).astype(bf16).astype(f32)
            flat[rows, :] = jnp.where(keep, updated, 0.0)
    out_ref[...] = flat[...].reshape(FIELDS * LEV, ROWS, BLOCK).astype(bf16)


def relax(fields, inverse, costs, lengths):
    vmem = pl.BlockSpec(memory_space=pltpu.VMEM)
    smem = pl.BlockSpec(memory_space=pltpu.SMEM)
    return pl.pallas_call(
        relax_kernel,
        out_shape=jax.ShapeDtypeStruct((FIELDS * LEV, ROWS, BLOCK), bf16),
        in_specs=[smem, smem, vmem, vmem],
        out_specs=vmem,
        scratch_shapes=[
            pltpu.VMEM((FIELDS * LEV * ROWS, BLOCK), f32),
            pltpu.VMEM((FIELDS, LEV, ROWS * BLOCK), bf16),
        ],
        compiler_params=pltpu.CompilerParams(vmem_limit_bytes=VMEM_BYTES),
        name="relax",
    )(costs, lengths, fields, inverse)


def fourier_kernel(x_ref, inner_ref, twiddle_ref, outer_ref, out_ref, flat):
    flat[...] = x_ref[...].astype(f32).reshape(N_COL * LEVELS * ROWS, BLOCK)
    inner = inner_ref[...]
    outer = outer_ref[...]

    @pl.loop(0, LEVELS)
    def _(i):
        for r in range(0, ROWS, 2):
            pair = [flat[pl.ds(i * ROWS + r + d, N_COL, stride=LEVELS * ROWS), :] for d in range(2)]
            x = jnp.concatenate(pair, axis=1).astype(bf16)
            y = jnp.dot(inner, jnp.concatenate([x, x], axis=0), preferred_element_type=f32)
            for d in range(2):
                lanes = slice(d * BLOCK, (d + 1) * BLOCK)
                real, imag = y[:N_COL, lanes], y[N_COL:, lanes]
                halves = []
                for h in range(2):
                    cosine = twiddle_ref[0, h * N_COL:(h + 1) * N_COL, :]
                    sine = twiddle_ref[1, h * N_COL:(h + 1) * N_COL, :]
                    halves.append(jnp.concatenate(
                        [(real * cosine + imag * sine).astype(bf16), (imag * cosine - real * sine).astype(bf16)], axis=1))
                z = jnp.concatenate(halves, axis=0)
                w = lax.dot_general(outer, z, (((1,), (1,)), ((), ())), preferred_element_type=f32)
                w = w[:2 * TILES] + w[2 * TILES:]
                for band in range(N_BAND):
                    out_ref[band, i, r + d] = w[band * 8:(band + 1) * 8].astype(bf16)


def fourier(pieces):
    inner, twiddle, outer = tables()
    vmem = pl.BlockSpec(memory_space=pltpu.VMEM)
    return pl.pallas_call(
        fourier_kernel,
        out_shape=jax.ShapeDtypeStruct((N_BAND, LEVELS, ROWS, 8, BLOCK), bf16),
        in_specs=[vmem] * 4,
        out_specs=vmem,
        scratch_shapes=[pltpu.VMEM((N_COL * LEVELS * ROWS, BLOCK), f32)],
        compiler_params=pltpu.CompilerParams(vmem_limit_bytes=VMEM_BYTES),
        name="fourier",
    )(pieces, jnp.asarray(inner), jnp.asarray(twiddle), jnp.asarray(outer))


def finish_kernel(x_ref, out_ref):
    for i in range(LEVELS):
        for band in range(N_BAND):
            for r in range(ROWS):
                piece = x_ref[band, i, r].astype(f32)
                for t in range(4):
                    out_ref[i, band * ROWS + r, :, t * BLOCK:(t + 1) * BLOCK] = piece[2 * t:2 * t + 2]


def finish(pieces):
    vmem = pl.BlockSpec(memory_space=pltpu.VMEM)
    return pl.pallas_call(
        finish_kernel,
        out_shape=jax.ShapeDtypeStruct((LEVELS, N_BAND * ROWS, 2, WAVES // N_BAND), f32),
        in_specs=[vmem],
        out_specs=vmem,
        compiler_params=pltpu.CompilerParams(vmem_limit_bytes=VMEM_BYTES),
        name="finish",
    )(pieces)


def shards(fields, inverse, block_costs, row_length):
    updated = relax(fields, inverse, block_costs, row_length)
    whole_rows = lax.all_to_all(updated, "col", split_axis=0, concat_axis=0, tiled=True)
    spectra = fourier(whole_rows)
    spectra = lax.all_to_all(spectra, "band", split_axis=0, concat_axis=0, tiled=True)
    return finish(spectra)


def solution(mesh):
    return jax.shard_map(
        shards,
        mesh=mesh,
        in_specs=(P(None, None, "band", "col"), P(), P("col", "band"), P("band")),
        out_specs=P("col", None, None, "band"),
        check_vma=False,
    )
```

```python
import math

import jax
import jax.numpy as jnp
import numpy as np
from jax import lax
from jax.experimental import pallas as pl
from jax.experimental.pallas import tpu as pltpu
from jax.sharding import Mesh, PartitionSpec as P

f32 = jnp.float32
bf16 = jnp.bfloat16
VMEM_BYTES = 40 * 1024 * 1024

FIELDS = 4
LEV = 80
ROWS = 8
BLOCK = 128
N_COL = 64
N_BAND = 4
NLON = N_COL * BLOCK
WAVES = 2048
TILES = WAVES // BLOCK
LEVELS = FIELDS * LEV // N_COL
COL_AXES = ("zhi", "y", "x", "core")
BAND_AXES = ("b1", "b0")
SEND_ORDER = ("y", "zhi", "x", "core")
SECTION = LEV // 2
SECTIONS = [y + 4 * zhi for y in range(4) for zhi in range(2)]
BANDS = [b0 + 2 * b1 for b0 in range(2) for b1 in range(2)]


def split_bf16(table):
    high = table.astype(np.float32).astype(jnp.bfloat16)
    low = (table - high.astype(np.float64)).astype(np.float32).astype(jnp.bfloat16)
    return high, low


def tables():
    q = np.arange(N_COL)
    source = np.concatenate([np.arange(8) + 8 * section for section in SECTIONS])
    angle = 2.0 * np.pi / N_COL * ((q[:, None] * source[None, :]) % N_COL)
    inner = np.concatenate([np.cos(angle), -np.sin(angle)], axis=0)
    inner = np.concatenate(split_bf16(inner), axis=1)
    u = np.arange(BLOCK)
    angle = 2.0 * np.pi / NLON * (u[:, None] * u[None, :])
    twiddle = np.stack([np.cos(angle), np.sin(angle)]).astype(np.float32)
    t = np.arange(TILES)
    angle = 2.0 * np.pi / (NLON // BLOCK) * ((t[:, None] * u[None, :]) % (NLON // BLOCK))
    cosine, sine = np.cos(angle), np.sin(angle)
    real_row = np.concatenate([cosine, sine], axis=1)
    imag_row = np.concatenate([-sine, cosine], axis=1)
    outer = np.stack([real_row, imag_row], axis=1).reshape(2 * TILES, 2 * BLOCK) / math.sqrt(NLON)
    outer = np.concatenate(split_bf16(outer), axis=0)
    outer = np.stack([outer[:, :BLOCK], outer[:, BLOCK:]])
    return inner, twiddle, outer


def relax_kernel(cost_ref, length_ref, fields_ref, inverse_ref, out_ref, flat, state):
    first = lax.axis_index(COL_AXES) * BLOCK
    flat[...] = fields_ref[...].astype(f32).reshape(FIELDS * LEV * ROWS, BLOCK)
    for f in range(FIELDS):
        for r in range(ROWS):
            piece = flat[pl.ds(f * LEV * ROWS + r, LEV, stride=ROWS), :]
            state[f, :, r * BLOCK:(r + 1) * BLOCK] = piece.astype(bf16)
    costs = [cost_ref[0, r] for r in range(ROWS)]
    most = costs[0]
    for r in range(1, ROWS):
        most = jnp.maximum(most, costs[r])
    cost_lanes = jnp.concatenate([jnp.full((1, BLOCK), costs[r], jnp.int32) for r in range(ROWS)], axis=1)

    @pl.loop(0, most)
    def _(s):
        active = s < cost_lanes
        for f in range(FIELDS):
            now = state[f]
            new = jnp.dot(inverse_ref[f], now, preferred_element_type=f32)
            state[f] = jnp.where(active, new, now.astype(f32)).astype(bf16)

    lane = first + lax.broadcasted_iota(jnp.int32, (1, BLOCK), 1)
    for r in range(ROWS):
        keep = lane < length_ref[r]
        for f in range(FIELDS):
            rows = pl.ds(f * LEV * ROWS + r, LEV, stride=ROWS)
            initial = flat[rows, :]
            relaxed = state[f, :, r * BLOCK:(r + 1) * BLOCK].astype(f32)
            tendency = (relaxed - initial).astype(bf16).astype(f32)
            updated = (initial + tendency).astype(bf16).astype(f32)
            flat[rows, :] = jnp.where(keep, updated, 0.0)
    for place, section in enumerate(SECTIONS):
        piece = flat[section * SECTION * ROWS:(section + 1) * SECTION * ROWS, :].reshape(SECTION, ROWS, BLOCK)
        out_ref[place * SECTION:(place + 1) * SECTION] = piece.astype(bf16)


def relax(fields, inverse, costs, lengths):
    vmem = pl.BlockSpec(memory_space=pltpu.VMEM)
    smem = pl.BlockSpec(memory_space=pltpu.SMEM)
    return pl.pallas_call(
        relax_kernel,
        out_shape=jax.ShapeDtypeStruct((FIELDS * LEV, ROWS, BLOCK), bf16),
        in_specs=[smem, smem, vmem, vmem],
        out_specs=vmem,
        scratch_shapes=[
            pltpu.VMEM((FIELDS * LEV * ROWS, BLOCK), f32),
            pltpu.VMEM((FIELDS, LEV, ROWS * BLOCK), bf16),
        ],
        compiler_params=pltpu.CompilerParams(vmem_limit_bytes=VMEM_BYTES),
        name="relax",
    )(costs, lengths, fields, inverse)


def fourier_kernel(x_ref, inner_ref, twiddle_ref, outer_ref, out_ref, flat):
    flat[...] = x_ref[...].astype(f32).reshape(N_COL * LEVELS * ROWS, BLOCK)
    inner = inner_ref[...]
    outer = jnp.concatenate([outer_ref[0], outer_ref[1]], axis=1)

    @pl.loop(0, LEVELS)
    def _(i):
        for r in range(0, ROWS, 2):
            pair = [flat[pl.ds(i * ROWS + r + d, N_COL, stride=LEVELS * ROWS), :] for d in range(2)]
            x = jnp.concatenate(pair, axis=1).astype(bf16)
            y = jnp.dot(inner, jnp.concatenate([x, x], axis=0), preferred_element_type=f32)
            for d in range(2):
                lanes = slice(d * BLOCK, (d + 1) * BLOCK)
                real, imag = y[:N_COL, lanes], y[N_COL:, lanes]
                halves = []
                for h in range(2):
                    cosine = twiddle_ref[0, h * N_COL:(h + 1) * N_COL, :]
                    sine = twiddle_ref[1, h * N_COL:(h + 1) * N_COL, :]
                    halves.append(jnp.concatenate(
                        [(real * cosine + imag * sine).astype(bf16), (imag * cosine - real * sine).astype(bf16)], axis=1))
                z = jnp.concatenate(halves, axis=0)
                w = lax.dot_general(outer, z, (((1,), (1,)), ((), ())), preferred_element_type=f32)
                w = w[:2 * TILES] + w[2 * TILES:]
                for place, band in enumerate(BANDS):
                    out_ref[place, i, r + d] = w[band * 8:(band + 1) * 8].astype(bf16)


def fourier(pieces):
    inner, twiddle, outer = tables()
    vmem = pl.BlockSpec(memory_space=pltpu.VMEM)
    return pl.pallas_call(
        fourier_kernel,
        out_shape=jax.ShapeDtypeStruct((N_BAND, LEVELS, ROWS, 8, BLOCK), bf16),
        in_specs=[vmem] * 4,
        out_specs=vmem,
        scratch_shapes=[pltpu.VMEM((N_COL * LEVELS * ROWS, BLOCK), f32)],
        compiler_params=pltpu.CompilerParams(vmem_limit_bytes=VMEM_BYTES),
        name="fourier",
    )(pieces, jnp.asarray(inner), jnp.asarray(twiddle), jnp.asarray(outer))


def finish_kernel(x_ref, out_ref):
    for i in range(LEVELS):
        for place, band in enumerate(BANDS):
            for r in range(ROWS):
                piece = x_ref[place, i, r].astype(f32)
                for t in range(4):
                    out_ref[i, band * ROWS + r, :, t * BLOCK:(t + 1) * BLOCK] = piece[2 * t:2 * t + 2]


def finish(pieces):
    vmem = pl.BlockSpec(memory_space=pltpu.VMEM)
    return pl.pallas_call(
        finish_kernel,
        out_shape=jax.ShapeDtypeStruct((LEVELS, N_BAND * ROWS, 2, WAVES // N_BAND), f32),
        in_specs=[vmem],
        out_specs=vmem,
        compiler_params=pltpu.CompilerParams(vmem_limit_bytes=VMEM_BYTES),
        name="finish",
    )(pieces)


def shards(fields, inverse, block_costs, row_length):
    updated = relax(fields, inverse, block_costs, row_length)
    whole_rows = lax.all_to_all(updated, SEND_ORDER, split_axis=0, concat_axis=0, tiled=True)
    spectra = fourier(whole_rows)
    spectra = lax.all_to_all(spectra, ("b0", "b1"), split_axis=0, concat_axis=0, tiled=True)
    return finish(spectra)


def solution(mesh):
    fine = Mesh(mesh.devices.reshape(2, 2, 2, 4, 4, 2), BAND_AXES + COL_AXES)
    return jax.shard_map(
        shards,
        mesh=fine,
        in_specs=(P(None, None, BAND_AXES, COL_AXES), P(), P(COL_AXES, BAND_AXES), P(BAND_AXES)),
        out_specs=P(COL_AXES, None, None, BAND_AXES),
        check_vma=False,
    )
```

```python
import functools
import math

import jax
import jax.numpy as jnp
import numpy as np
from jax import lax
from jax.experimental import pallas as pl
from jax.experimental.pallas import tpu as pltpu
from jax.sharding import Mesh, PartitionSpec as P

f32 = jnp.float32
bf16 = jnp.bfloat16
VMEM_BYTES = 40 * 1024 * 1024

FIELDS = 4
LEV = 80
ROWS = 8
BLOCK = 128
N_COL = 64
N_BAND = 4
NLON = N_COL * BLOCK
WAVES = 2048
LEVELS = FIELDS * LEV // N_COL
COL_AXES = ("zhi", "y", "x", "core")
HALF = N_COL // 2


def split_bf16(table):
    high = table.astype(np.float32).astype(jnp.bfloat16)
    low = (table - high.astype(np.float64)).astype(np.float32).astype(jnp.bfloat16)
    return high, low


def tables():
    q = np.arange(N_COL)
    s = np.arange(HALF)
    angle = 2.0 * np.pi / N_COL * ((q[:, None] * s[None, :]) % N_COL)
    inner = np.concatenate([np.cos(angle), -np.sin(angle)], axis=0)
    sign = np.where(np.arange(2 * N_COL) % 2 == 0, 1.0, -1.0)
    inner = np.stack([inner, inner * sign[:, None]])
    inner = np.concatenate(split_bf16(inner), axis=2)
    b = np.arange(BLOCK)
    angle = 2.0 * np.pi / NLON * (q[:, None] * b[None, :])
    twiddle = np.stack([np.cos(angle), np.sin(angle)]).astype(np.float32)
    p = np.arange(WAVES // N_COL).reshape(-1, 2).T.reshape(-1)
    angle = 2.0 * np.pi / BLOCK * ((p[:, None] * b[None, :]) % BLOCK)
    cosine, sine = np.cos(angle), np.sin(angle)
    real_row = np.concatenate([cosine, sine], axis=1)
    imag_row = np.concatenate([-sine, cosine], axis=1)
    outer = np.stack([real_row, imag_row], axis=1).reshape(2 * WAVES // N_COL, 2 * BLOCK) / math.sqrt(NLON)
    outer = np.concatenate(split_bf16(outer), axis=0)
    outer = np.stack([outer[:, :BLOCK], outer[:, BLOCK:]])
    return inner, twiddle, outer


def relax_kernel(cost_ref, length_ref, fields_ref, inverse_ref, out_ref, flat, state):
    first = lax.axis_index(COL_AXES) * BLOCK
    flat[...] = fields_ref[...].astype(f32).reshape(FIELDS * LEV * ROWS, BLOCK)
    for f in range(FIELDS):
        for r in range(ROWS):
            piece = flat[pl.ds(f * LEV * ROWS + r, LEV, stride=ROWS), :]
            state[f, :, r * BLOCK:(r + 1) * BLOCK] = piece.astype(bf16)
    costs = [cost_ref[0, r] for r in range(ROWS)]
    most = costs[0]
    for r in range(1, ROWS):
        most = jnp.maximum(most, costs[r])
    cost_lanes = jnp.concatenate([jnp.full((1, BLOCK), costs[r], jnp.int32) for r in range(ROWS)], axis=1)

    @pl.loop(0, most)
    def _(s):
        active = s < cost_lanes
        for f in range(FIELDS):
            now = state[f]
            new = jnp.dot(inverse_ref[f], now, preferred_element_type=f32)
            state[f] = jnp.where(active, new, now.astype(f32)).astype(bf16)

    lane = first + lax.broadcasted_iota(jnp.int32, (1, BLOCK), 1)
    for r in range(ROWS):
        keep = lane < length_ref[r]
        for f in range(FIELDS):
            rows = pl.ds(f * LEV * ROWS + r, LEV, stride=ROWS)
            initial = flat[rows, :]
            relaxed = state[f, :, r * BLOCK:(r + 1) * BLOCK].astype(f32)
            tendency = (relaxed - initial).astype(bf16).astype(f32)
            updated = (initial + tendency).astype(bf16).astype(f32)
            flat[rows, :] = jnp.where(keep, updated, 0.0)
    span = HALF * LEVELS
    for h in range(2):
        piece = flat[h * span * ROWS:(h + 1) * span * ROWS, :].reshape(HALF, LEVELS, ROWS, BLOCK)
        out_ref[:, h] = piece.astype(bf16)


def relax(fields, inverse, costs, lengths):
    vmem = pl.BlockSpec(memory_space=pltpu.VMEM)
    smem = pl.BlockSpec(memory_space=pltpu.SMEM)
    return pl.pallas_call(
        relax_kernel,
        out_shape=jax.ShapeDtypeStruct((HALF, 2, LEVELS, ROWS, BLOCK), bf16),
        in_specs=[smem, smem, vmem, vmem],
        out_specs=vmem,
        scratch_shapes=[
            pltpu.VMEM((FIELDS * LEV * ROWS, BLOCK), f32),
            pltpu.VMEM((FIELDS, LEV, ROWS * BLOCK), bf16),
        ],
        compiler_params=pltpu.CompilerParams(vmem_limit_bytes=VMEM_BYTES),
        name="relax",
    )(costs, lengths, fields, inverse)


def fourier_kernel(own, x_ref, inner_ref, twiddle_ref, outer_ref, out_ref, flat):
    half = lax.axis_index("zhi")
    band = lax.axis_index("band")
    part = half if own else 1 - half
    flat[...] = x_ref[:, part].astype(f32).reshape(HALF * LEVELS * ROWS, BLOCK)
    inner = inner_ref[half]
    outer = jnp.concatenate([outer_ref[0], outer_ref[1]], axis=1)
    cosine, sine = twiddle_ref[0], twiddle_ref[1]
    left = lax.broadcasted_iota(jnp.int32, (1, BLOCK), 1) < N_COL
    place = [lax.rem(to + N_BAND - band, N_BAND) for to in range(N_BAND)]
    waves = WAVES // N_COL

    @pl.loop(0, LEVELS)
    def _(i):
        for r in range(0, ROWS, 4):
            twisted = []
            for e in range(r, r + 4, 2):
                pair = [flat[pl.ds(i * ROWS + e + d, HALF, stride=LEVELS * ROWS), :] for d in range(2)]
                x = jnp.concatenate(pair, axis=1).astype(bf16)
                y = jnp.dot(inner, jnp.concatenate([x, x], axis=0), preferred_element_type=f32)
                for d in range(2):
                    lanes = slice(d * BLOCK, (d + 1) * BLOCK)
                    real, imag = y[:N_COL, lanes], y[N_COL:, lanes]
                    twisted.append(jnp.concatenate(
                        [(real * cosine + imag * sine).astype(bf16), (imag * cosine - real * sine).astype(bf16)], axis=1))
            z = jnp.concatenate(twisted, axis=0)
            w = lax.dot_general(outer, z, (((1,), (1,)), ((), ())), preferred_element_type=f32)
            w = w[:2 * waves] + w[2 * waves:]
            for k in range(2):
                even = w[:waves, k * BLOCK:(k + 1) * BLOCK]
                odd = w[waves:, k * BLOCK:(k + 1) * BLOCK]
                rows = (jnp.where(left, even, pltpu.roll(odd, N_COL, 1)), jnp.where(left, pltpu.roll(even, N_COL, 1), odd))
                for d in range(2):
                    for to in range(N_BAND):
                        out_ref[place[to], i, r + 2 * k + d] = rows[d][to * 8:(to + 1) * 8].astype(bf16)


def fourier(pieces, own):
    inner, twiddle, outer = tables()
    vmem = pl.BlockSpec(memory_space=pltpu.VMEM)
    return pl.pallas_call(
        functools.partial(fourier_kernel, own),
        out_shape=jax.ShapeDtypeStruct((N_BAND, LEVELS, ROWS, 8, BLOCK), bf16),
        in_specs=[vmem] * 4,
        out_specs=vmem,
        scratch_shapes=[pltpu.VMEM((HALF * LEVELS * ROWS, BLOCK), f32)],
        compiler_params=pltpu.CompilerParams(vmem_limit_bytes=VMEM_BYTES),
        cost_estimate=pl.CostEstimate(flops=3_000_000_000, bytes_accessed=1_000_000, transcendentals=0),
        name="fourier_own" if own else "fourier_other",
    )(pieces, jnp.asarray(inner), jnp.asarray(twiddle), jnp.asarray(outer))


def finish_kernel(own_ref, *refs):
    ours, theirs, out_ref = refs[:N_BAND - 1], refs[N_BAND - 1:-1], refs[-1]
    band = lax.axis_index("band")
    for shift in range(N_BAND):
        first = lax.rem(band + N_BAND - shift, N_BAND) * ROWS
        for i in range(LEVELS):
            for r in range(ROWS):
                near = own_ref[0, i, r] if shift == 0 else ours[shift - 1][i, r]
                piece = near.astype(f32) + theirs[shift][i, r].astype(f32)
                for t in range(4):
                    out_ref[i, first + r, :, t * BLOCK:(t + 1) * BLOCK] = piece[2 * t:2 * t + 2]


def finish(own, ours, theirs):
    vmem = pl.BlockSpec(memory_space=pltpu.VMEM)
    return pl.pallas_call(
        finish_kernel,
        out_shape=jax.ShapeDtypeStruct((LEVELS, N_BAND * ROWS, 2, WAVES // N_BAND), f32),
        in_specs=[vmem] * (2 * N_BAND),
        out_specs=vmem,
        compiler_params=pltpu.CompilerParams(vmem_limit_bytes=VMEM_BYTES),
        name="finish",
    )(own, *ours, *theirs)


def along_z(piece, flip, shift):
    pairs = []
    for band in range(N_BAND):
        for half in range(2):
            pairs.append((band * 2 + half, (band + shift) % N_BAND * 2 + (half ^ flip)))
    return lax.ppermute(piece, ("band", "zhi"), pairs)


def shards(fields, inverse, block_costs, row_length):
    updated = relax(fields, inverse, block_costs, row_length)
    half_rows = lax.all_to_all(updated, ("y", "x", "core"), split_axis=0, concat_axis=0, tiled=True)
    other = fourier(half_rows, False)
    theirs = [along_z(other[shift], 1, shift) for shift in range(N_BAND)]
    own = fourier(half_rows, True)
    ours = [along_z(own[shift], 0, shift) for shift in range(1, N_BAND)]
    return finish(own, ours, theirs)


def solution(mesh):
    fine = Mesh(mesh.devices.reshape(N_BAND, 2, 4, 4, 2), ("band",) + COL_AXES)
    return jax.shard_map(
        shards,
        mesh=fine,
        in_specs=(P(None, None, "band", COL_AXES), P(), P(COL_AXES, "band"), P("band")),
        out_specs=P(COL_AXES, None, None, "band"),
        check_vma=False,
    )
```

```python
import functools
import math

import jax
import jax.numpy as jnp
import numpy as np
from jax import lax
from jax.experimental import pallas as pl
from jax.experimental.pallas import tpu as pltpu
from jax.sharding import Mesh, PartitionSpec as P

f32 = jnp.float32
bf16 = jnp.bfloat16
VMEM_BYTES = 40 * 1024 * 1024
RELAX_BYTES = 61 * 1024 * 1024

FIELDS = 4
LEV = 80
ROWS = 8
BLOCK = 128
N_COL = 64
N_BAND = 4
NLON = N_COL * BLOCK
WAVES = 2048
LEVELS = FIELDS * LEV // N_COL
COL_AXES = ("zhi", "y", "x", "core")
HALF = N_COL // 2


def split_bf16(table):
    high = table.astype(np.float32).astype(jnp.bfloat16)
    low = (table - high.astype(np.float64)).astype(np.float32).astype(jnp.bfloat16)
    return high, low


def tables():
    q = np.arange(N_COL)
    s = np.arange(HALF)
    angle = 2.0 * np.pi / N_COL * ((q[:, None] * s[None, :]) % N_COL)
    inner = np.concatenate([np.cos(angle), -np.sin(angle)], axis=0)
    sign = np.where(np.arange(2 * N_COL) % 2 == 0, 1.0, -1.0)
    inner = np.stack([inner, inner * sign[:, None]])
    inner = np.concatenate(split_bf16(inner), axis=2)
    b = np.arange(BLOCK)
    angle = 2.0 * np.pi / NLON * (q[:, None] * b[None, :])
    twiddle = np.stack([np.cos(angle), np.sin(angle)]).astype(np.float32)
    p = np.arange(WAVES // N_COL).reshape(-1, 2).T.reshape(-1)
    angle = 2.0 * np.pi / BLOCK * ((p[:, None] * b[None, :]) % BLOCK)
    cosine, sine = np.cos(angle), np.sin(angle)
    real_row = np.concatenate([cosine, sine], axis=1)
    imag_row = np.concatenate([-sine, cosine], axis=1)
    outer = np.stack([real_row, imag_row], axis=1).reshape(2 * WAVES // N_COL, 2 * BLOCK) / math.sqrt(NLON)
    outer = np.concatenate(split_bf16(outer), axis=0)
    outer = np.stack([outer[:, :BLOCK], outer[:, BLOCK:]])
    return inner, twiddle, outer


def relax_kernel(
    cost_hbm, length_hbm, fields_hbm, inverse_hbm, out_hbm,
    cost_ref, length_ref, fields_ref, inverse_ref, flat, state, start, out_ref, sems, out_sems,
):
    copies = [pltpu.make_async_copy(fields_hbm.at[f], fields_ref.at[f], sems.at[f]) for f in range(FIELDS)]
    small = [
        pltpu.make_async_copy(inverse_hbm, inverse_ref, sems.at[FIELDS]),
        pltpu.make_async_copy(cost_hbm, cost_ref, sems.at[FIELDS + 1]),
        pltpu.make_async_copy(length_hbm, length_ref, sems.at[FIELDS + 2]),
    ]
    for copy in copies + small:
        copy.start()
    first = lax.axis_index(COL_AXES) * BLOCK
    for f in range(FIELDS):
        copies[f].wait()
        flat[f * LEV * ROWS:(f + 1) * LEV * ROWS, :] = fields_ref[f].astype(f32).reshape(LEV * ROWS, BLOCK)
        for r in range(ROWS):
            piece = flat[pl.ds(f * LEV * ROWS + r, LEV, stride=ROWS), :].astype(bf16)
            state[f, :, r * BLOCK:(r + 1) * BLOCK] = piece
            start[f, :, r * BLOCK:(r + 1) * BLOCK] = piece
    for copy in small:
        copy.wait()
    costs = [cost_ref[0, r] for r in range(ROWS)]
    most = costs[0]
    for r in range(1, ROWS):
        most = jnp.maximum(most, costs[r])
    cost_lanes = jnp.concatenate([jnp.full((1, BLOCK), costs[r], jnp.int32) for r in range(ROWS)], axis=1)

    @pl.loop(0, most)
    def _(s):
        active = s < cost_lanes
        for f in range(FIELDS):
            now = state[f]
            new = jnp.dot(inverse_ref[f], now, preferred_element_type=f32)
            state[f] = jnp.where(active, new, now.astype(f32)).astype(bf16)

    lane = first + lax.broadcasted_iota(jnp.int32, (1, BLOCK), 1)
    keep = [lane < length_ref[r] for r in range(ROWS)]
    sends = []
    for f in range(FIELDS):
        for r in range(ROWS):
            lanes = slice(r * BLOCK, (r + 1) * BLOCK)
            initial = start[f, :, lanes].astype(f32)
            relaxed = state[f, :, lanes].astype(f32)
            tendency = (relaxed - initial).astype(bf16).astype(f32)
            updated = (initial + tendency).astype(bf16).astype(f32)
            flat[pl.ds(f * LEV * ROWS + r, LEV, stride=ROWS), :] = jnp.where(keep[r], updated, 0.0)
        piece = flat[f * LEV * ROWS:(f + 1) * LEV * ROWS, :].reshape(LEV // LEVELS, LEVELS, ROWS, BLOCK)
        out_ref[f] = piece.astype(bf16)
        first = f % 2 * (LEV // LEVELS)
        sends.append(pltpu.make_async_copy(out_ref.at[f], out_hbm.at[pl.ds(first, LEV // LEVELS), f // 2], out_sems.at[f]))
        sends[-1].start()
    for send in sends:
        send.wait()


def relax(fields, inverse, costs, lengths):
    return pl.pallas_call(
        relax_kernel,
        out_shape=jax.ShapeDtypeStruct((HALF, 2, LEVELS, ROWS, BLOCK), bf16),
        in_specs=[pl.BlockSpec(memory_space=pltpu.HBM)] * 4,
        out_specs=pl.BlockSpec(memory_space=pltpu.HBM),
        scratch_shapes=[
            pltpu.SMEM((1, ROWS), jnp.int32),
            pltpu.SMEM((ROWS,), jnp.int32),
            pltpu.VMEM((FIELDS, LEV, ROWS, BLOCK), bf16),
            pltpu.VMEM((FIELDS, LEV, LEV), bf16),
            pltpu.VMEM((FIELDS * LEV * ROWS, BLOCK), f32),
            pltpu.VMEM((FIELDS, LEV, ROWS * BLOCK), bf16),
            pltpu.VMEM((FIELDS, LEV, ROWS * BLOCK), bf16),
            pltpu.VMEM((FIELDS, LEV // LEVELS, LEVELS, ROWS, BLOCK), bf16),
            pltpu.SemaphoreType.DMA((FIELDS + 3,)),
            pltpu.SemaphoreType.DMA((FIELDS,)),
        ],
        compiler_params=pltpu.CompilerParams(vmem_limit_bytes=RELAX_BYTES),
        name="relax",
    )(costs, lengths, fields, inverse)


def fourier_kernel(own, x_ref, inner_ref, twiddle_ref, outer_ref, out_ref, flat):
    half = lax.axis_index("zhi")
    band = lax.axis_index("band")
    part = half if own else 1 - half
    flat[...] = x_ref[:, part].astype(f32).reshape(HALF * LEVELS * ROWS, BLOCK)
    inner = inner_ref[half]
    outer = jnp.concatenate([outer_ref[0], outer_ref[1]], axis=1)
    cosine, sine = twiddle_ref[0], twiddle_ref[1]
    left = lax.broadcasted_iota(jnp.int32, (1, BLOCK), 1) < N_COL
    place = [lax.rem(to + N_BAND - band, N_BAND) for to in range(N_BAND)]
    waves = WAVES // N_COL

    @pl.loop(0, LEVELS)
    def _(i):
        for r in range(0, ROWS, 4):
            twisted = []
            for e in range(r, r + 4, 2):
                pair = [flat[pl.ds(i * ROWS + e + d, HALF, stride=LEVELS * ROWS), :] for d in range(2)]
                x = jnp.concatenate(pair, axis=1).astype(bf16)
                y = jnp.dot(inner, jnp.concatenate([x, x], axis=0), preferred_element_type=f32)
                for d in range(2):
                    lanes = slice(d * BLOCK, (d + 1) * BLOCK)
                    real, imag = y[:N_COL, lanes], y[N_COL:, lanes]
                    twisted.append(jnp.concatenate(
                        [(real * cosine + imag * sine).astype(bf16), (imag * cosine - real * sine).astype(bf16)], axis=1))
            z = jnp.concatenate(twisted, axis=0)
            w = lax.dot_general(outer, z, (((1,), (1,)), ((), ())), preferred_element_type=f32)
            w = w[:2 * waves] + w[2 * waves:]
            for k in range(2):
                even = w[:waves, k * BLOCK:(k + 1) * BLOCK]
                odd = w[waves:, k * BLOCK:(k + 1) * BLOCK]
                rows = (jnp.where(left, even, pltpu.roll(odd, N_COL, 1)), jnp.where(left, pltpu.roll(even, N_COL, 1), odd))
                for d in range(2):
                    for to in range(N_BAND):
                        out_ref[place[to], i, r + 2 * k + d] = rows[d][to * 8:(to + 1) * 8].astype(bf16)


def fourier(pieces, own):
    inner, twiddle, outer = tables()
    vmem = pl.BlockSpec(memory_space=pltpu.VMEM)
    return pl.pallas_call(
        functools.partial(fourier_kernel, own),
        out_shape=jax.ShapeDtypeStruct((N_BAND, LEVELS, ROWS, 8, BLOCK), bf16),
        in_specs=[vmem] * 4,
        out_specs=vmem,
        scratch_shapes=[pltpu.VMEM((HALF * LEVELS * ROWS, BLOCK), f32)],
        compiler_params=pltpu.CompilerParams(vmem_limit_bytes=VMEM_BYTES),
        cost_estimate=pl.CostEstimate(flops=3_000_000_000, bytes_accessed=1_000_000, transcendentals=0),
        name="fourier_own" if own else "fourier_other",
    )(pieces, jnp.asarray(inner), jnp.asarray(twiddle), jnp.asarray(outer))


def finish_kernel(own_ref, *refs):
    ours, theirs = refs[:N_BAND - 1], refs[N_BAND - 1:2 * N_BAND - 1]
    out_hbm, buffer, sems = refs[2 * N_BAND - 1:]
    band = lax.axis_index("band")
    copies = []
    for shift in range(N_BAND):
        first = lax.rem(band + N_BAND - shift, N_BAND) * ROWS
        for i in range(LEVELS):
            for r in range(ROWS):
                near = own_ref[0, i, r] if shift == 0 else ours[shift - 1][i, r]
                piece = near.astype(f32) + theirs[shift][i, r].astype(f32)
                for t in range(4):
                    buffer[shift, i, r, :, t * BLOCK:(t + 1) * BLOCK] = piece[2 * t:2 * t + 2]
        copies.append(pltpu.make_async_copy(buffer.at[shift], out_hbm.at[:, pl.ds(first, ROWS)], sems.at[shift]))
        copies[-1].start()
    for copy in copies:
        copy.wait()


def finish(own, ours, theirs):
    vmem = pl.BlockSpec(memory_space=pltpu.VMEM)
    return pl.pallas_call(
        finish_kernel,
        out_shape=jax.ShapeDtypeStruct((LEVELS, N_BAND * ROWS, 2, WAVES // N_BAND), f32),
        in_specs=[vmem] * (2 * N_BAND),
        out_specs=pl.BlockSpec(memory_space=pltpu.HBM),
        scratch_shapes=[
            pltpu.VMEM((N_BAND, LEVELS, ROWS, 2, WAVES // N_BAND), f32),
            pltpu.SemaphoreType.DMA((N_BAND,)),
        ],
        compiler_params=pltpu.CompilerParams(vmem_limit_bytes=VMEM_BYTES),
        name="finish",
    )(own, *ours, *theirs)


def along_z(piece, flip, shift):
    pairs = []
    for band in range(N_BAND):
        for half in range(2):
            pairs.append((band * 2 + half, (band + shift) % N_BAND * 2 + (half ^ flip)))
    return lax.ppermute(piece, ("band", "zhi"), pairs)


def shards(fields, inverse, block_costs, row_length):
    updated = relax(fields, inverse, block_costs, row_length)
    half_rows = lax.all_to_all(updated, ("y", "x", "core"), split_axis=0, concat_axis=0, tiled=True)
    other = fourier(half_rows, False)
    theirs = [along_z(other[shift], 1, shift) for shift in range(N_BAND)]
    own = fourier(half_rows, True)
    ours = [along_z(own[shift], 0, shift) for shift in range(1, N_BAND)]
    return finish(own, ours, theirs)


def solution(mesh):
    fine = Mesh(mesh.devices.reshape(N_BAND, 2, 4, 4, 2), ("band",) + COL_AXES)
    return jax.shard_map(
        shards,
        mesh=fine,
        in_specs=(P(None, None, "band", COL_AXES), P(), P(COL_AXES, "band"), P("band")),
        out_specs=P(COL_AXES, None, None, "band"),
        check_vma=False,
    )
```

```python
import math

import jax
import jax.numpy as jnp
import numpy as np
from jax import lax
from jax.experimental import pallas as pl
from jax.experimental.pallas import tpu as pltpu
from jax.sharding import Mesh, PartitionSpec as P

f32 = jnp.float32
bf16 = jnp.bfloat16
VMEM_BYTES = 40 * 1024 * 1024
RELAX_BYTES = 61 * 1024 * 1024

FIELDS = 4
LEV = 80
ROWS = 8
BLOCK = 128
N_COL = 64
N_BAND = 4
NLON = N_COL * BLOCK
WAVES = 2048
LEVELS = FIELDS * LEV // N_COL
COL_AXES = ("zhi", "y", "x", "core")
HALF = N_COL // 2
PAIRS = N_COL // 4
PAIR = 2 * LEVELS


def split_bf16(table):
    high = table.astype(np.float32).astype(jnp.bfloat16)
    low = (table - high.astype(np.float64)).astype(np.float32).astype(jnp.bfloat16)
    return high, low


def tables():
    q = np.arange(N_COL)
    s = np.arange(HALF)
    angle = 2.0 * np.pi / N_COL * ((q[:, None] * s[None, :]) % N_COL)
    inner = np.concatenate([np.cos(angle), -np.sin(angle)], axis=0)
    sign = np.where(np.arange(2 * N_COL) % 2 == 0, 1.0, -1.0)
    inner = np.stack([inner, inner * sign[:, None]])
    inner = np.concatenate(split_bf16(inner), axis=2)
    b = np.arange(BLOCK)
    angle = 2.0 * np.pi / NLON * (q[:, None] * b[None, :])
    twiddle = np.stack([np.cos(angle), np.sin(angle)]).astype(np.float32)
    p = np.arange(WAVES // N_COL).reshape(-1, 2).T.reshape(-1)
    angle = 2.0 * np.pi / BLOCK * ((p[:, None] * b[None, :]) % BLOCK)
    cosine, sine = np.cos(angle), np.sin(angle)
    real_row = np.concatenate([cosine, sine], axis=1)
    imag_row = np.concatenate([-sine, cosine], axis=1)
    outer = np.stack([real_row, imag_row], axis=1).reshape(2 * WAVES // N_COL, 2 * BLOCK) / math.sqrt(NLON)
    outer = np.concatenate(split_bf16(outer), axis=0)
    outer = np.stack([outer[:, :BLOCK], outer[:, BLOCK:]])
    return inner, twiddle, outer


def relax_kernel(
    cost_hbm, length_hbm, fields_hbm, inverse_hbm, out_hbm,
    cost_ref, length_ref, fields_ref, inverse_ref, flat, state, start, out_ref, sems, out_sems,
):
    copies = [pltpu.make_async_copy(fields_hbm.at[f], fields_ref.at[f], sems.at[f]) for f in range(FIELDS)]
    small = [
        pltpu.make_async_copy(inverse_hbm, inverse_ref, sems.at[FIELDS]),
        pltpu.make_async_copy(cost_hbm, cost_ref, sems.at[FIELDS + 1]),
        pltpu.make_async_copy(length_hbm, length_ref, sems.at[FIELDS + 2]),
    ]
    for copy in copies + small:
        copy.start()
    first = lax.axis_index(COL_AXES) * BLOCK
    for f in range(FIELDS):
        copies[f].wait()
        flat[f * LEV * ROWS:(f + 1) * LEV * ROWS, :] = fields_ref[f].astype(f32).reshape(LEV * ROWS, BLOCK)
        for r in range(ROWS):
            piece = flat[pl.ds(f * LEV * ROWS + r, LEV, stride=ROWS), :].astype(bf16)
            state[f, :, r * BLOCK:(r + 1) * BLOCK] = piece
            start[f, :, r * BLOCK:(r + 1) * BLOCK] = piece
    for copy in small:
        copy.wait()
    costs = [cost_ref[0, r] for r in range(ROWS)]
    most = costs[0]
    for r in range(1, ROWS):
        most = jnp.maximum(most, costs[r])
    cost_lanes = jnp.concatenate([jnp.full((16, BLOCK), costs[r], jnp.int32) for r in range(ROWS)], axis=1).astype(f32).astype(bf16)

    @pl.loop(0, most)
    def _(s):
        step = jnp.full((16, ROWS * BLOCK), s, jnp.int32).astype(f32).astype(bf16)
        active = jnp.concatenate([cost_lanes > step] * (LEV // 16), axis=0)
        for f in range(FIELDS):
            now = state[f]
            new = jnp.dot(inverse_ref[f], now, preferred_element_type=f32)
            state[f] = jnp.where(active, new.astype(bf16), now)

    lane = first + lax.broadcasted_iota(jnp.int32, (1, BLOCK), 1)
    keep = [lane < length_ref[r] for r in range(ROWS)]
    sends = []
    for f in range(FIELDS):
        for r in range(ROWS):
            lanes = slice(r * BLOCK, (r + 1) * BLOCK)
            initial = start[f, :, lanes].astype(f32)
            relaxed = state[f, :, lanes].astype(f32)
            tendency = (relaxed - initial).astype(bf16).astype(f32)
            updated = (initial + tendency).astype(bf16).astype(f32)
            flat[pl.ds(f * LEV * ROWS + r, LEV, stride=ROWS), :] = jnp.where(keep[r], updated, 0.0)
        piece = flat[f * LEV * ROWS:(f + 1) * LEV * ROWS, :].reshape(LEV // PAIR, PAIR, ROWS, BLOCK)
        out_ref[f] = piece.astype(bf16)
        first = f % 2 * (LEV // PAIR)
        sends.append(pltpu.make_async_copy(out_ref.at[f], out_hbm.at[pl.ds(first, LEV // PAIR), f // 2], out_sems.at[f]))
        sends[-1].start()
    for send in sends:
        send.wait()


def relax(fields, inverse, costs, lengths):
    return pl.pallas_call(
        relax_kernel,
        out_shape=jax.ShapeDtypeStruct((PAIRS, 2, PAIR, ROWS, BLOCK), bf16),
        in_specs=[pl.BlockSpec(memory_space=pltpu.HBM)] * 4,
        out_specs=pl.BlockSpec(memory_space=pltpu.HBM),
        scratch_shapes=[
            pltpu.SMEM((1, ROWS), jnp.int32),
            pltpu.SMEM((ROWS,), jnp.int32),
            pltpu.VMEM((FIELDS, LEV, ROWS, BLOCK), bf16),
            pltpu.VMEM((FIELDS, LEV, LEV), bf16),
            pltpu.VMEM((FIELDS * LEV * ROWS, BLOCK), f32),
            pltpu.VMEM((FIELDS, LEV, ROWS * BLOCK), bf16),
            pltpu.VMEM((FIELDS, LEV, ROWS * BLOCK), bf16),
            pltpu.VMEM((FIELDS, LEV // PAIR, PAIR, ROWS, BLOCK), bf16),
            pltpu.SemaphoreType.DMA((FIELDS + 3,)),
            pltpu.SemaphoreType.DMA((FIELDS,)),
        ],
        compiler_params=pltpu.CompilerParams(vmem_limit_bytes=RELAX_BYTES),
        name="relax",
    )(costs, lengths, fields, inverse)


def fourier_kernel(x_ref, inner_ref, twiddle_ref, outer_ref, out_ref, flat):
    half = lax.axis_index("zhi")
    band = lax.axis_index("band")
    inner = inner_ref[half]
    outer = jnp.concatenate([outer_ref[0], outer_ref[1]], axis=1)
    cosine, sine = twiddle_ref[0], twiddle_ref[1]
    left = lax.broadcasted_iota(jnp.int32, (1, BLOCK), 1) < N_COL
    place = [lax.rem(to + N_BAND - band, N_BAND) for to in range(N_BAND)]
    waves = WAVES // N_COL

    def load(i, slot):
        flat[slot] = x_ref[:, i].astype(f32).reshape(HALF * ROWS, BLOCK)

    def transform(i, buffer):
        core = lax.div(i, LEVELS)
        level = i - core * LEVELS
        slot = lax.rem(core + half, 2)
        for r in range(0, ROWS, 4):
            twisted = []
            for e in range(r, r + 4, 2):
                pair = [flat[buffer, pl.ds(e + d, HALF, stride=ROWS), :] for d in range(2)]
                x = jnp.concatenate(pair, axis=1).astype(bf16)
                y = jnp.dot(inner, jnp.concatenate([x, x], axis=0), preferred_element_type=f32)
                for d in range(2):
                    lanes = slice(d * BLOCK, (d + 1) * BLOCK)
                    real, imag = y[:N_COL, lanes], y[N_COL:, lanes]
                    twisted.append(jnp.concatenate(
                        [(real * cosine + imag * sine).astype(bf16), (imag * cosine - real * sine).astype(bf16)], axis=1))
            z = jnp.concatenate(twisted, axis=0)
            w = lax.dot_general(outer, z, (((1,), (1,)), ((), ())), preferred_element_type=f32)
            w = w[:2 * waves] + w[2 * waves:]
            for k in range(4 // 2):
                even = w[:waves, k * BLOCK:(k + 1) * BLOCK]
                odd = w[waves:, k * BLOCK:(k + 1) * BLOCK]
                rows = (jnp.where(left, even, pltpu.roll(odd, N_COL, 1)), jnp.where(left, pltpu.roll(even, N_COL, 1), odd))
                for d in range(2):
                    for to in range(N_BAND):
                        out_ref[place[to], slot, level, r + 2 * k + d] = rows[d][to * 8:(to + 1) * 8].astype(bf16)

    load(0, 0)

    @pl.loop(0, PAIR // 2)
    def _(j):
        load(2 * j + 1, 1)
        transform(2 * j, 0)
        load(jnp.minimum(2 * j + 2, PAIR - 1), 0)
        transform(2 * j + 1, 1)


def fourier(pieces):
    inner, twiddle, outer = tables()
    vmem = pl.BlockSpec(memory_space=pltpu.VMEM)
    return pl.pallas_call(
        fourier_kernel,
        out_shape=jax.ShapeDtypeStruct((N_BAND, 2, LEVELS, ROWS, 8, BLOCK), bf16),
        in_specs=[vmem] * 4,
        out_specs=vmem,
        scratch_shapes=[pltpu.VMEM((2, HALF * ROWS, BLOCK), f32)],
        compiler_params=pltpu.CompilerParams(vmem_limit_bytes=VMEM_BYTES),
        name="fourier",
    )(pieces, jnp.asarray(inner), jnp.asarray(twiddle), jnp.asarray(outer))


def finish_kernel(*refs):
    ours, theirs = refs[:N_BAND], refs[N_BAND:2 * N_BAND]
    out_hbm, buffer, sems = refs[2 * N_BAND:]
    band = lax.axis_index("band")
    copies = []
    for shift in range(N_BAND):
        first = lax.rem(band + N_BAND - shift, N_BAND) * ROWS
        for i in range(LEVELS):
            for r in range(ROWS):
                piece = ours[shift][0, i, r].astype(f32) + theirs[shift][i, r].astype(f32)
                for t in range(4):
                    buffer[shift, i, r, :, t * BLOCK:(t + 1) * BLOCK] = piece[2 * t:2 * t + 2]
        copies.append(pltpu.make_async_copy(buffer.at[shift], out_hbm.at[:, pl.ds(first, ROWS)], sems.at[shift]))
        copies[-1].start()
    for copy in copies:
        copy.wait()


def finish(ours, theirs):
    vmem = pl.BlockSpec(memory_space=pltpu.VMEM)
    return pl.pallas_call(
        finish_kernel,
        out_shape=jax.ShapeDtypeStruct((LEVELS, N_BAND * ROWS, 2, WAVES // N_BAND), f32),
        in_specs=[vmem] * (2 * N_BAND),
        out_specs=pl.BlockSpec(memory_space=pltpu.HBM),
        scratch_shapes=[
            pltpu.VMEM((N_BAND, LEVELS, ROWS, 2, WAVES // N_BAND), f32),
            pltpu.SemaphoreType.DMA((N_BAND,)),
        ],
        compiler_params=pltpu.CompilerParams(vmem_limit_bytes=VMEM_BYTES),
        name="finish",
    )(*ours, *theirs)


def along_z(piece, shift):
    pairs = []
    for band in range(N_BAND):
        for half in range(2):
            for core in range(2):
                to = ((band + shift) % N_BAND * 2 + core) * 2 + half
                pairs.append(((band * 2 + half) * 2 + core, to))
    return lax.ppermute(piece, ("band", "zhi", "core"), pairs)


def shards(fields, inverse, block_costs, row_length):
    updated = relax(fields, inverse, block_costs, row_length)
    half_rows = lax.all_to_all(
        updated.reshape(HALF, PAIR, ROWS, BLOCK), ("y", "x", "core"), split_axis=0, concat_axis=0, tiled=True
    )
    spectra = fourier(half_rows)
    ours = [along_z(spectra[shift], shift) for shift in range(N_BAND)]
    theirs = [lax.ppermute(piece[1], "core", [(0, 1), (1, 0)]) for piece in ours]
    return finish(ours, theirs)


def solution(mesh):
    fine = Mesh(mesh.devices.reshape(N_BAND, 2, 4, 4, 2), ("band",) + COL_AXES)
    return jax.shard_map(
        shards,
        mesh=fine,
        in_specs=(P(None, None, "band", COL_AXES), P(), P(COL_AXES, "band"), P("band")),
        out_specs=P(COL_AXES, None, None, "band"),
        check_vma=False,
    )
```

```python
import math

import jax
import jax.numpy as jnp
import numpy as np
from jax import lax
from jax.experimental import pallas as pl
from jax.experimental.pallas import tpu as pltpu
from jax.sharding import Mesh, PartitionSpec as P

f32 = jnp.float32
bf16 = jnp.bfloat16
VMEM_BYTES = 40 * 1024 * 1024
RELAX_BYTES = 61 * 1024 * 1024

FIELDS = 4
LEV = 80
CMAX = 8
ROWS = 8
BLOCK = 128
N_COL = 64
N_BAND = 4
NLON = N_COL * BLOCK
WAVES = 2048
LEVELS = FIELDS * LEV // N_COL
COL_AXES = ("zhi", "y", "x", "core")
HALF = N_COL // 2
PAIRS = N_COL // 4
PAIR = 2 * LEVELS


def split_bf16(table):
    high = table.astype(np.float32).astype(jnp.bfloat16)
    low = (table - high.astype(np.float64)).astype(np.float32).astype(jnp.bfloat16)
    return high, low


def tables():
    q = np.arange(N_COL)
    s = np.arange(HALF)
    angle = 2.0 * np.pi / N_COL * ((q[:, None] * s[None, :]) % N_COL)
    inner = np.concatenate([np.cos(angle), -np.sin(angle)], axis=0)
    sign = np.where(np.arange(2 * N_COL) % 2 == 0, 1.0, -1.0)
    inner = np.stack([inner, inner * sign[:, None]])
    inner = np.concatenate(split_bf16(inner), axis=2)
    b = np.arange(BLOCK)
    angle = 2.0 * np.pi / NLON * (q[:, None] * b[None, :])
    twiddle = np.stack([np.cos(angle), np.sin(angle)]).astype(np.float32)
    p = np.arange(WAVES // N_COL).reshape(-1, 2).T.reshape(-1)
    angle = 2.0 * np.pi / BLOCK * ((p[:, None] * b[None, :]) % BLOCK)
    cosine, sine = np.cos(angle), np.sin(angle)
    real_row = np.concatenate([cosine, sine], axis=1)
    imag_row = np.concatenate([-sine, cosine], axis=1)
    outer = np.stack([real_row, imag_row], axis=1).reshape(2 * WAVES // N_COL, 2 * BLOCK) / math.sqrt(NLON)
    outer = np.concatenate(split_bf16(outer), axis=0)
    outer = np.stack([outer[:, :BLOCK], outer[:, BLOCK:]])
    return inner, twiddle, outer


def relax_kernel(
    cost_hbm, length_hbm, fields_hbm, inverse_hbm, out_hbm,
    cost_ref, length_ref, fields_ref, inverse_ref, flat, state, start, out_ref, sems, out_sems,
):
    copies = [pltpu.make_async_copy(fields_hbm.at[f], fields_ref.at[f], sems.at[f]) for f in range(FIELDS)]
    small = [
        pltpu.make_async_copy(inverse_hbm, inverse_ref, sems.at[FIELDS]),
        pltpu.make_async_copy(cost_hbm, cost_ref, sems.at[FIELDS + 1]),
        pltpu.make_async_copy(length_hbm, length_ref, sems.at[FIELDS + 2]),
    ]
    for copy in copies + small:
        copy.start()
    first = lax.axis_index(COL_AXES) * BLOCK
    for f in range(FIELDS):
        copies[f].wait()
        flat[f * LEV * ROWS:(f + 1) * LEV * ROWS, :] = fields_ref[f].astype(f32).reshape(LEV * ROWS, BLOCK)
        for r in range(ROWS):
            piece = flat[pl.ds(f * LEV * ROWS + r, LEV, stride=ROWS), :].astype(bf16)
            state[f, :, r * BLOCK:(r + 1) * BLOCK] = piece
            start[f, :, r * BLOCK:(r + 1) * BLOCK] = piece
    for copy in small:
        copy.wait()
    costs = [cost_ref[0, r] for r in range(ROWS)]
    most = costs[0]
    for r in range(1, ROWS):
        most = jnp.maximum(most, costs[r])
    cost_lanes = jnp.concatenate([jnp.full((16, BLOCK), costs[r], jnp.int32) for r in range(ROWS)], axis=1).astype(f32).astype(bf16)

    def sweep(s):
        step = jnp.full((16, ROWS * BLOCK), s, jnp.int32).astype(f32).astype(bf16)
        for f in range(FIELDS):
            for t in range(0, ROWS * BLOCK, 2 * BLOCK):
                active = jnp.concatenate([cost_lanes[:, t:t + 2 * BLOCK] > step[:, t:t + 2 * BLOCK]] * (LEV // 16), axis=0)
                now = state[f, :, t:t + 2 * BLOCK]
                new = jnp.dot(inverse_ref[f], now, preferred_element_type=f32)
                state[f, :, t:t + 2 * BLOCK] = jnp.where(active, new.astype(bf16), now)

    sweep(0)

    @pl.when(most > 1)
    def _():
        for s in range(1, CMAX):
            sweep(s)

    lane = first + lax.broadcasted_iota(jnp.int32, (1, BLOCK), 1)
    keep = [lane < length_ref[r] for r in range(ROWS)]
    sends = []
    for f in range(FIELDS):
        for r in range(ROWS):
            lanes = slice(r * BLOCK, (r + 1) * BLOCK)
            initial = start[f, :, lanes].astype(f32)
            relaxed = state[f, :, lanes].astype(f32)
            tendency = (relaxed - initial).astype(bf16).astype(f32)
            updated = (initial + tendency).astype(bf16).astype(f32)
            flat[pl.ds(f * LEV * ROWS + r, LEV, stride=ROWS), :] = jnp.where(keep[r], updated, 0.0)
        piece = flat[f * LEV * ROWS:(f + 1) * LEV * ROWS, :].reshape(LEV // PAIR, PAIR, ROWS, BLOCK)
        out_ref[f] = piece.astype(bf16)
        first = f % 2 * (LEV // PAIR)
        sends.append(pltpu.make_async_copy(out_ref.at[f], out_hbm.at[pl.ds(first, LEV // PAIR), f // 2], out_sems.at[f]))
        sends[-1].start()
    for send in sends:
        send.wait()


def relax(fields, inverse, costs, lengths):
    return pl.pallas_call(
        relax_kernel,
        out_shape=jax.ShapeDtypeStruct((PAIRS, 2, PAIR, ROWS, BLOCK), bf16),
        in_specs=[pl.BlockSpec(memory_space=pltpu.HBM)] * 4,
        out_specs=pl.BlockSpec(memory_space=pltpu.HBM),
        scratch_shapes=[
            pltpu.SMEM((1, ROWS), jnp.int32),
            pltpu.SMEM((ROWS,), jnp.int32),
            pltpu.VMEM((FIELDS, LEV, ROWS, BLOCK), bf16),
            pltpu.VMEM((FIELDS, LEV, LEV), bf16),
            pltpu.VMEM((FIELDS * LEV * ROWS, BLOCK), f32),
            pltpu.VMEM((FIELDS, LEV, ROWS * BLOCK), bf16),
            pltpu.VMEM((FIELDS, LEV, ROWS * BLOCK), bf16),
            pltpu.VMEM((FIELDS, LEV // PAIR, PAIR, ROWS, BLOCK), bf16),
            pltpu.SemaphoreType.DMA((FIELDS + 3,)),
            pltpu.SemaphoreType.DMA((FIELDS,)),
        ],
        compiler_params=pltpu.CompilerParams(vmem_limit_bytes=RELAX_BYTES),
        name="relax",
    )(costs, lengths, fields, inverse)


def fourier_kernel(x_ref, inner_ref, twiddle_ref, outer_ref, out_ref, flat):
    half = lax.axis_index("zhi")
    band = lax.axis_index("band")
    inner = inner_ref[half]
    outer = jnp.concatenate([outer_ref[0], outer_ref[1]], axis=1)
    cosine, sine = twiddle_ref[0], twiddle_ref[1]
    left = lax.broadcasted_iota(jnp.int32, (1, BLOCK), 1) < N_COL
    place = [lax.rem(to + N_BAND - band, N_BAND) for to in range(N_BAND)]
    waves = WAVES // N_COL

    def load(i, slot):
        flat[slot] = x_ref[:, i].astype(f32).reshape(HALF * ROWS, BLOCK)

    def transform(i, buffer):
        core = lax.div(i, LEVELS)
        level = i - core * LEVELS
        slot = lax.rem(core + half, 2)
        for r in range(0, ROWS, 4):
            twisted = []
            for e in range(r, r + 4, 2):
                pair = [flat[buffer, pl.ds(e + d, HALF, stride=ROWS), :] for d in range(2)]
                x = jnp.concatenate(pair, axis=1).astype(bf16)
                y = jnp.dot(inner, jnp.concatenate([x, x], axis=0), preferred_element_type=f32)
                for d in range(2):
                    lanes = slice(d * BLOCK, (d + 1) * BLOCK)
                    real, imag = y[:N_COL, lanes], y[N_COL:, lanes]
                    twisted.append(jnp.concatenate(
                        [(real * cosine + imag * sine).astype(bf16), (imag * cosine - real * sine).astype(bf16)], axis=1))
            z = jnp.concatenate(twisted, axis=0)
            w = lax.dot_general(outer, z, (((1,), (1,)), ((), ())), preferred_element_type=f32)
            w = w[:2 * waves] + w[2 * waves:]
            for k in range(4 // 2):
                even = w[:waves, k * BLOCK:(k + 1) * BLOCK]
                odd = w[waves:, k * BLOCK:(k + 1) * BLOCK]
                rows = (jnp.where(left, even, pltpu.roll(odd, N_COL, 1)), jnp.where(left, pltpu.roll(even, N_COL, 1), odd))
                for d in range(2):
                    for to in range(N_BAND):
                        out_ref[place[to], slot, level, r + 2 * k + d] = rows[d][to * 8:(to + 1) * 8].astype(bf16)

    load(0, 0)

    @pl.loop(0, PAIR // 2)
    def _(j):
        load(2 * j + 1, 1)
        transform(2 * j, 0)
        load(jnp.minimum(2 * j + 2, PAIR - 1), 0)
        transform(2 * j + 1, 1)


def fourier(pieces):
    inner, twiddle, outer = tables()
    vmem = pl.BlockSpec(memory_space=pltpu.VMEM)
    return pl.pallas_call(
        fourier_kernel,
        out_shape=jax.ShapeDtypeStruct((N_BAND, 2, LEVELS, ROWS, 8, BLOCK), bf16),
        in_specs=[vmem] * 4,
        out_specs=vmem,
        scratch_shapes=[pltpu.VMEM((2, HALF * ROWS, BLOCK), f32)],
        compiler_params=pltpu.CompilerParams(vmem_limit_bytes=VMEM_BYTES),
        name="fourier",
    )(pieces, jnp.asarray(inner), jnp.asarray(twiddle), jnp.asarray(outer))


def finish_kernel(*refs):
    ours, theirs = refs[:N_BAND], refs[N_BAND:2 * N_BAND]
    out_hbm, buffer, sems = refs[2 * N_BAND:]
    band = lax.axis_index("band")
    copies = []
    for shift in range(N_BAND):
        first = lax.rem(band + N_BAND - shift, N_BAND) * ROWS
        for i in range(LEVELS):
            for r in range(ROWS):
                piece = ours[shift][0, i, r].astype(f32) + theirs[shift][i, r].astype(f32)
                for t in range(4):
                    buffer[shift, i, r, :, t * BLOCK:(t + 1) * BLOCK] = piece[2 * t:2 * t + 2]
        copies.append(pltpu.make_async_copy(buffer.at[shift], out_hbm.at[:, pl.ds(first, ROWS)], sems.at[shift]))
        copies[-1].start()
    for copy in copies:
        copy.wait()


def finish(ours, theirs):
    vmem = pl.BlockSpec(memory_space=pltpu.VMEM)
    return pl.pallas_call(
        finish_kernel,
        out_shape=jax.ShapeDtypeStruct((LEVELS, N_BAND * ROWS, 2, WAVES // N_BAND), f32),
        in_specs=[vmem] * (2 * N_BAND),
        out_specs=pl.BlockSpec(memory_space=pltpu.HBM),
        scratch_shapes=[
            pltpu.VMEM((N_BAND, LEVELS, ROWS, 2, WAVES // N_BAND), f32),
            pltpu.SemaphoreType.DMA((N_BAND,)),
        ],
        compiler_params=pltpu.CompilerParams(vmem_limit_bytes=VMEM_BYTES),
        name="finish",
    )(*ours, *theirs)


def along_z(piece, shift):
    pairs = []
    for band in range(N_BAND):
        for half in range(2):
            for core in range(2):
                to = ((band + shift) % N_BAND * 2 + core) * 2 + half
                pairs.append(((band * 2 + half) * 2 + core, to))
    return lax.ppermute(piece, ("band", "zhi", "core"), pairs)


def shards(fields, inverse, block_costs, row_length):
    updated = relax(fields, inverse, block_costs, row_length)
    half_rows = lax.all_to_all(
        updated.reshape(HALF, PAIR, ROWS, BLOCK), ("y", "x", "core"), split_axis=0, concat_axis=0, tiled=True
    )
    spectra = fourier(half_rows)
    ours = [along_z(spectra[shift], shift) for shift in range(N_BAND)]
    theirs = [lax.ppermute(piece[1], "core", [(0, 1), (1, 0)]) for piece in ours]
    return finish(ours, theirs)


def solution(mesh):
    fine = Mesh(mesh.devices.reshape(N_BAND, 2, 4, 4, 2), ("band",) + COL_AXES)
    return jax.shard_map(
        shards,
        mesh=fine,
        in_specs=(P(None, None, "band", COL_AXES), P(), P(COL_AXES, "band"), P("band")),
        out_specs=P(COL_AXES, None, None, "band"),
        check_vma=False,
    )
```

```python
import functools
import math

import jax
import jax.numpy as jnp
import numpy as np
from jax import lax
from jax.experimental import pallas as pl
from jax.experimental.pallas import tpu as pltpu
from jax.sharding import Mesh, PartitionSpec as P

f32 = jnp.float32
bf16 = jnp.bfloat16
VMEM_BYTES = 40 * 1024 * 1024
RELAX_BYTES = 61 * 1024 * 1024

FIELDS = 4
LEV = 80
CMAX = 8
ROWS = 8
BLOCK = 128
N_COL = 64
N_BAND = 4
NLON = N_COL * BLOCK
WAVES = 2048
LEVELS = FIELDS * LEV // N_COL
COL_AXES = ("zhi", "y", "x", "core")
HALF = N_COL // 2
PAIRS = N_COL // 4
PAIR = 2 * LEVELS


def split_bf16(table):
    high = table.astype(np.float32).astype(jnp.bfloat16)
    low = (table - high.astype(np.float64)).astype(np.float32).astype(jnp.bfloat16)
    return high, low


def tables():
    q = np.arange(N_COL)
    s = np.arange(HALF)
    angle = 2.0 * np.pi / N_COL * ((q[:, None] * s[None, :]) % N_COL)
    inner = np.concatenate([np.cos(angle), -np.sin(angle)], axis=0)
    sign = np.where(np.arange(2 * N_COL) % 2 == 0, 1.0, -1.0)
    inner = np.stack([inner, inner * sign[:, None]])
    inner = np.concatenate(split_bf16(inner), axis=2)
    b = np.arange(BLOCK)
    angle = 2.0 * np.pi / NLON * (q[:, None] * b[None, :])
    twiddle = np.stack([np.cos(angle), np.sin(angle)]).astype(np.float32)
    p = np.arange(WAVES // N_COL).reshape(-1, 2).T.reshape(-1)
    angle = 2.0 * np.pi / BLOCK * ((p[:, None] * b[None, :]) % BLOCK)
    cosine, sine = np.cos(angle), np.sin(angle)
    real_row = np.concatenate([cosine, sine], axis=1)
    imag_row = np.concatenate([-sine, cosine], axis=1)
    outer = np.stack([real_row, imag_row], axis=1).reshape(2 * WAVES // N_COL, 2 * BLOCK) / math.sqrt(NLON)
    outer = np.concatenate(split_bf16(outer), axis=0)
    outer = np.stack([outer[:, :BLOCK], outer[:, BLOCK:]])
    return inner, twiddle, outer


def relax_kernel(
    cost_hbm, length_hbm, fields_hbm, inverse_hbm, out_hbm,
    cost_ref, length_ref, fields_ref, inverse_ref, flat, state, start, out_ref, sems, out_sems,
):
    copies = [pltpu.make_async_copy(fields_hbm.at[f], fields_ref.at[f], sems.at[f]) for f in range(FIELDS)]
    small = [
        pltpu.make_async_copy(inverse_hbm, inverse_ref, sems.at[FIELDS]),
        pltpu.make_async_copy(cost_hbm, cost_ref, sems.at[FIELDS + 1]),
        pltpu.make_async_copy(length_hbm, length_ref, sems.at[FIELDS + 2]),
    ]
    for copy in copies + small:
        copy.start()
    first = lax.axis_index(COL_AXES) * BLOCK
    for f in range(FIELDS):
        copies[f].wait()
        flat[f * LEV * ROWS:(f + 1) * LEV * ROWS, :] = fields_ref[f].astype(f32).reshape(LEV * ROWS, BLOCK)
        for r in range(ROWS):
            piece = flat[pl.ds(f * LEV * ROWS + r, LEV, stride=ROWS), :].astype(bf16)
            state[f, :, r * BLOCK:(r + 1) * BLOCK] = piece
            start[f, :, r * BLOCK:(r + 1) * BLOCK] = piece
    for copy in small:
        copy.wait()
    costs = [cost_ref[0, r] for r in range(ROWS)]
    most = costs[0]
    for r in range(1, ROWS):
        most = jnp.maximum(most, costs[r])
    cost_lanes = jnp.concatenate([jnp.full((16, BLOCK), costs[r], jnp.int32) for r in range(ROWS)], axis=1).astype(f32).astype(bf16)

    def sweep(s):
        step = jnp.full((16, ROWS * BLOCK), s, jnp.int32).astype(f32).astype(bf16)
        for f in range(FIELDS):
            for t in range(0, ROWS * BLOCK, 2 * BLOCK):
                active = jnp.concatenate([cost_lanes[:, t:t + 2 * BLOCK] > step[:, t:t + 2 * BLOCK]] * (LEV // 16), axis=0)
                now = state[f, :, t:t + 2 * BLOCK]
                new = jnp.dot(inverse_ref[f], now, preferred_element_type=f32)
                state[f, :, t:t + 2 * BLOCK] = jnp.where(active, new.astype(bf16), now)

    sweep(0)

    @pl.when(most > 1)
    def _():
        for s in range(1, CMAX):
            sweep(s)

    lane = first + lax.broadcasted_iota(jnp.int32, (1, BLOCK), 1)
    keep = [lane < length_ref[r] for r in range(ROWS)]
    sends = []
    for f in range(FIELDS):
        for r in range(ROWS):
            lanes = slice(r * BLOCK, (r + 1) * BLOCK)
            initial = start[f, :, lanes].astype(f32)
            relaxed = state[f, :, lanes].astype(f32)
            tendency = (relaxed - initial).astype(bf16).astype(f32)
            updated = (initial + tendency).astype(bf16).astype(f32)
            flat[pl.ds(f * LEV * ROWS + r, LEV, stride=ROWS), :] = jnp.where(keep[r], updated, 0.0)
        piece = flat[f * LEV * ROWS:(f + 1) * LEV * ROWS, :].reshape(LEV // PAIR, PAIR, ROWS, BLOCK)
        out_ref[f] = piece.astype(bf16)
        first = f % 2 * (LEV // PAIR)
        sends.append(pltpu.make_async_copy(out_ref.at[f], out_hbm.at[pl.ds(first, LEV // PAIR), f // 2], out_sems.at[f]))
        sends[-1].start()
    for send in sends:
        send.wait()


def relax(fields, inverse, costs, lengths):
    return pl.pallas_call(
        relax_kernel,
        out_shape=jax.ShapeDtypeStruct((PAIRS, 2, PAIR, ROWS, BLOCK), bf16),
        in_specs=[pl.BlockSpec(memory_space=pltpu.HBM)] * 4,
        out_specs=pl.BlockSpec(memory_space=pltpu.HBM),
        scratch_shapes=[
            pltpu.SMEM((1, ROWS), jnp.int32),
            pltpu.SMEM((ROWS,), jnp.int32),
            pltpu.VMEM((FIELDS, LEV, ROWS, BLOCK), bf16),
            pltpu.VMEM((FIELDS, LEV, LEV), bf16),
            pltpu.VMEM((FIELDS * LEV * ROWS, BLOCK), f32),
            pltpu.VMEM((FIELDS, LEV, ROWS * BLOCK), bf16),
            pltpu.VMEM((FIELDS, LEV, ROWS * BLOCK), bf16),
            pltpu.VMEM((FIELDS, LEV // PAIR, PAIR, ROWS, BLOCK), bf16),
            pltpu.SemaphoreType.DMA((FIELDS + 3,)),
            pltpu.SemaphoreType.DMA((FIELDS,)),
        ],
        compiler_params=pltpu.CompilerParams(vmem_limit_bytes=RELAX_BYTES),
        name="relax",
    )(costs, lengths, fields, inverse)


def fourier_kernel(x_ref, inner_ref, twiddle_ref, outer_ref, out_ref, flat):
    half = lax.axis_index("zhi")
    band = lax.axis_index("band")
    inner = inner_ref[half]
    outer = jnp.concatenate([outer_ref[0], outer_ref[1]], axis=1)
    cosine, sine = twiddle_ref[0], twiddle_ref[1]
    left = lax.broadcasted_iota(jnp.int32, (1, BLOCK), 1) < N_COL
    place = [lax.rem(to + N_BAND - band, N_BAND) for to in range(N_BAND)]
    waves = WAVES // N_COL

    def load(i, slot):
        flat[slot] = x_ref[:, i].astype(f32).reshape(HALF * ROWS, BLOCK)

    def transform(i, buffer):
        core, level = divmod(i, LEVELS)
        slot = lax.rem(core + half, 2)
        for r in range(0, ROWS, 4):
            twisted = []
            for e in range(r, r + 4, 2):
                pair = [flat[buffer, pl.ds(e + d, HALF, stride=ROWS), :] for d in range(2)]
                x = jnp.concatenate(pair, axis=1).astype(bf16)
                y = jnp.dot(inner, jnp.concatenate([x, x], axis=0), preferred_element_type=f32)
                for d in range(2):
                    lanes = slice(d * BLOCK, (d + 1) * BLOCK)
                    real, imag = y[:N_COL, lanes], y[N_COL:, lanes]
                    twisted.append(jnp.concatenate(
                        [(real * cosine + imag * sine).astype(bf16), (imag * cosine - real * sine).astype(bf16)], axis=1))
            z = jnp.concatenate(twisted, axis=0)
            w = lax.dot_general(outer, z, (((1,), (1,)), ((), ())), preferred_element_type=f32)
            w = w[:2 * waves] + w[2 * waves:]
            for k in range(4 // 2):
                even = w[:waves, k * BLOCK:(k + 1) * BLOCK]
                odd = w[waves:, k * BLOCK:(k + 1) * BLOCK]
                rows = (jnp.where(left, even, pltpu.roll(odd, N_COL, 1)), jnp.where(left, pltpu.roll(even, N_COL, 1), odd))
                for d in range(2):
                    for to in range(N_BAND):
                        out_ref[place[to], slot, level, r + 2 * k + d] = rows[d][to * 8:(to + 1) * 8].astype(bf16)

    load(0, 0)
    for i in range(PAIR):
        if i + 1 < PAIR:
            load(i + 1, (i + 1) % 2)
        transform(i, i % 2)


def fourier(pieces):
    inner, twiddle, outer = tables()
    vmem = pl.BlockSpec(memory_space=pltpu.VMEM)
    return pl.pallas_call(
        fourier_kernel,
        out_shape=jax.ShapeDtypeStruct((N_BAND, 2, LEVELS, ROWS, 8, BLOCK), bf16),
        in_specs=[vmem] * 4,
        out_specs=vmem,
        scratch_shapes=[pltpu.VMEM((2, HALF * ROWS, BLOCK), f32)],
        compiler_params=pltpu.CompilerParams(vmem_limit_bytes=VMEM_BYTES),
        name="fourier",
    )(pieces, jnp.asarray(inner), jnp.asarray(twiddle), jnp.asarray(outer))


def finish_kernel(shifts, *refs):
    count = len(shifts)
    ours, theirs = refs[:count], refs[count:2 * count]
    out_hbm, buffer, sems = refs[-3:]
    band = lax.axis_index("band")
    copies = []
    for k, shift in enumerate(shifts):
        first = lax.rem(band + N_BAND - shift, N_BAND) * ROWS
        for i in range(LEVELS):
            for r in range(ROWS):
                piece = ours[k][0, i, r].astype(f32) + theirs[k][i, r].astype(f32)
                for t in range(4):
                    buffer[k, i, r, :, t * BLOCK:(t + 1) * BLOCK] = piece[2 * t:2 * t + 2]
        copies.append(pltpu.make_async_copy(buffer.at[k], out_hbm.at[:, pl.ds(first, ROWS)], sems.at[k]))
        copies[-1].start()
    for copy in copies:
        copy.wait()


def finish(shifts, ours, theirs, before=None):
    vmem = pl.BlockSpec(memory_space=pltpu.VMEM)
    hbm = pl.BlockSpec(memory_space=pltpu.HBM)
    count = len(shifts)
    rest = [] if before is None else [before]
    return pl.pallas_call(
        functools.partial(finish_kernel, shifts),
        out_shape=jax.ShapeDtypeStruct((LEVELS, N_BAND * ROWS, 2, WAVES // N_BAND), f32),
        in_specs=[vmem] * (2 * count) + [hbm] * len(rest),
        out_specs=hbm,
        scratch_shapes=[
            pltpu.VMEM((count, LEVELS, ROWS, 2, WAVES // N_BAND), f32),
            pltpu.SemaphoreType.DMA((count,)),
        ],
        input_output_aliases={2 * count: 0} if rest else {},
        compiler_params=pltpu.CompilerParams(vmem_limit_bytes=VMEM_BYTES),
        name="finish",
    )(*[ours[shift] for shift in shifts], *[theirs[shift] for shift in shifts], *rest)


def along_z(piece, shift):
    pairs = []
    for band in range(N_BAND):
        for half in range(2):
            for core in range(2):
                to = ((band + shift) % N_BAND * 2 + core) * 2 + half
                pairs.append(((band * 2 + half) * 2 + core, to))
    return lax.ppermute(piece, ("band", "zhi", "core"), pairs)


def shards(fields, inverse, block_costs, row_length):
    updated = relax(fields, inverse, block_costs, row_length)
    half_rows = lax.all_to_all(
        updated.reshape(HALF, PAIR, ROWS, BLOCK), ("y", "x", "core"), split_axis=0, concat_axis=0, tiled=True
    )
    spectra = fourier(half_rows)
    ours = [along_z(spectra[shift], shift) for shift in range(N_BAND)]
    theirs = [lax.ppermute(piece[1], "core", [(0, 1), (1, 0)]) for piece in ours]
    return finish((3,), ours, theirs, finish((0, 1, 2), ours, theirs))


def solution(mesh):
    fine = Mesh(mesh.devices.reshape(N_BAND, 2, 4, 4, 2), ("band",) + COL_AXES)
    return jax.shard_map(
        shards,
        mesh=fine,
        in_specs=(P(None, None, "band", COL_AXES), P(), P(COL_AXES, "band"), P("band")),
        out_specs=P(COL_AXES, None, None, "band"),
        check_vma=False,
    )
```

```python
import functools
import math

import jax
import jax.numpy as jnp
import numpy as np
from jax import lax
from jax.experimental import pallas as pl
from jax.experimental.pallas import tpu as pltpu
from jax.sharding import Mesh, PartitionSpec as P

f32 = jnp.float32
bf16 = jnp.bfloat16
VMEM_BYTES = 40 * 1024 * 1024
RELAX_BYTES = 61 * 1024 * 1024

FIELDS = 4
LEV = 80
CMAX = 8
ROWS = 8
BLOCK = 128
N_COL = 64
N_BAND = 4
NLON = N_COL * BLOCK
WAVES = 2048
LEVELS = FIELDS * LEV // N_COL
COL_AXES = ("zhi", "y", "x", "core")
HALF = N_COL // 2
PAIRS = N_COL // 4
PAIR = 2 * LEVELS


def split_bf16(table):
    high = table.astype(np.float32).astype(jnp.bfloat16)
    low = (table - high.astype(np.float64)).astype(np.float32).astype(jnp.bfloat16)
    return high, low


def tables():
    q = np.arange(N_COL)
    s = np.arange(HALF).reshape(PAIRS, 2).T.reshape(-1)
    angle = 2.0 * np.pi / N_COL * ((q[:, None] * s[None, :]) % N_COL)
    inner = np.concatenate([np.cos(angle), -np.sin(angle)], axis=0)
    sign = np.where(np.arange(2 * N_COL) % 2 == 0, 1.0, -1.0)
    inner = np.stack([inner, inner * sign[:, None]])
    inner = np.concatenate(split_bf16(inner), axis=2)
    b = np.arange(BLOCK)
    angle = 2.0 * np.pi / NLON * (q[:, None] * b[None, :])
    twiddle = np.stack([np.cos(angle), np.sin(angle)]).astype(np.float32)
    p = np.arange(WAVES // N_COL).reshape(-1, 2).T.reshape(-1)
    angle = 2.0 * np.pi / BLOCK * ((p[:, None] * b[None, :]) % BLOCK)
    cosine, sine = np.cos(angle), np.sin(angle)
    real_row = np.concatenate([cosine, sine], axis=1)
    imag_row = np.concatenate([-sine, cosine], axis=1)
    outer = np.stack([real_row, imag_row], axis=1).reshape(2 * WAVES // N_COL, 2 * BLOCK) / math.sqrt(NLON)
    outer = np.concatenate(split_bf16(outer), axis=0)
    outer = np.stack([outer[:, :BLOCK], outer[:, BLOCK:]])
    return inner, twiddle, outer


def relax_kernel(
    cost_hbm, length_hbm, fields_hbm, inverse_hbm, out_hbm,
    cost_ref, length_ref, fields_ref, inverse_ref, flat, state, start, out_ref, sems, out_sems,
):
    copies = [pltpu.make_async_copy(fields_hbm.at[f], fields_ref.at[f], sems.at[f]) for f in range(FIELDS)]
    small = [
        pltpu.make_async_copy(inverse_hbm, inverse_ref, sems.at[FIELDS]),
        pltpu.make_async_copy(cost_hbm, cost_ref, sems.at[FIELDS + 1]),
        pltpu.make_async_copy(length_hbm, length_ref, sems.at[FIELDS + 2]),
    ]
    for copy in copies + small:
        copy.start()
    first = lax.axis_index(COL_AXES) * BLOCK
    for f in range(FIELDS):
        copies[f].wait()
        flat[f * LEV * ROWS:(f + 1) * LEV * ROWS, :] = fields_ref[f].astype(f32).reshape(LEV * ROWS, BLOCK)
        for r in range(ROWS):
            piece = flat[pl.ds(f * LEV * ROWS + r, LEV, stride=ROWS), :].astype(bf16)
            state[f, :, r * BLOCK:(r + 1) * BLOCK] = piece
            start[f, :, r * BLOCK:(r + 1) * BLOCK] = piece
    for copy in small:
        copy.wait()
    costs = [cost_ref[0, r] for r in range(ROWS)]
    most = costs[0]
    for r in range(1, ROWS):
        most = jnp.maximum(most, costs[r])
    cost_lanes = jnp.concatenate([jnp.full((16, BLOCK), costs[r], jnp.int32) for r in range(ROWS)], axis=1).astype(f32).astype(bf16)

    def sweep(s):
        step = jnp.full((16, ROWS * BLOCK), s, jnp.int32).astype(f32).astype(bf16)
        for f in range(FIELDS):
            for t in range(0, ROWS * BLOCK, 2 * BLOCK):
                active = jnp.concatenate([cost_lanes[:, t:t + 2 * BLOCK] > step[:, t:t + 2 * BLOCK]] * (LEV // 16), axis=0)
                now = state[f, :, t:t + 2 * BLOCK]
                new = jnp.dot(inverse_ref[f], now, preferred_element_type=f32)
                state[f, :, t:t + 2 * BLOCK] = jnp.where(active, new.astype(bf16), now)

    sweep(0)

    @pl.when(most > 1)
    def _():
        for s in range(1, CMAX):
            sweep(s)

    lane = first + lax.broadcasted_iota(jnp.int32, (1, BLOCK), 1)
    keep = [lane < length_ref[r] for r in range(ROWS)]
    sends = []
    for f in range(FIELDS):
        for r in range(ROWS):
            lanes = slice(r * BLOCK, (r + 1) * BLOCK)
            initial = start[f, :, lanes].astype(f32)
            relaxed = state[f, :, lanes].astype(f32)
            tendency = (relaxed - initial).astype(bf16).astype(f32)
            updated = (initial + tendency).astype(bf16).astype(f32)
            flat[pl.ds(f * LEV * ROWS + r, LEV, stride=ROWS), :] = jnp.where(keep[r], updated, 0.0)
        piece = flat[f * LEV * ROWS:(f + 1) * LEV * ROWS, :].reshape(LEV // PAIR, PAIR, ROWS, BLOCK)
        out_ref[f] = piece.astype(bf16)
        first = f % 2 * (LEV // PAIR)
        sends.append(pltpu.make_async_copy(out_ref.at[f], out_hbm.at[f // 2, pl.ds(first, LEV // PAIR)], out_sems.at[f]))
        sends[-1].start()
    for send in sends:
        send.wait()


def relax(fields, inverse, costs, lengths):
    return pl.pallas_call(
        relax_kernel,
        out_shape=jax.ShapeDtypeStruct((2, PAIRS, PAIR, ROWS, BLOCK), bf16),
        in_specs=[pl.BlockSpec(memory_space=pltpu.HBM)] * 4,
        out_specs=pl.BlockSpec(memory_space=pltpu.HBM),
        scratch_shapes=[
            pltpu.SMEM((1, ROWS), jnp.int32),
            pltpu.SMEM((ROWS,), jnp.int32),
            pltpu.VMEM((FIELDS, LEV, ROWS, BLOCK), bf16),
            pltpu.VMEM((FIELDS, LEV, LEV), bf16),
            pltpu.VMEM((FIELDS * LEV * ROWS, BLOCK), f32),
            pltpu.VMEM((FIELDS, LEV, ROWS * BLOCK), bf16),
            pltpu.VMEM((FIELDS, LEV, ROWS * BLOCK), bf16),
            pltpu.VMEM((FIELDS, LEV // PAIR, PAIR, ROWS, BLOCK), bf16),
            pltpu.SemaphoreType.DMA((FIELDS + 3,)),
            pltpu.SemaphoreType.DMA((FIELDS,)),
        ],
        compiler_params=pltpu.CompilerParams(vmem_limit_bytes=RELAX_BYTES),
        name="relax",
    )(costs, lengths, fields, inverse)


def fourier_kernel(x_ref, inner_ref, twiddle_ref, outer_ref, out_ref, flat):
    half = lax.axis_index("zhi")
    band = lax.axis_index("band")
    inner = inner_ref[half]
    outer = jnp.concatenate([outer_ref[0], outer_ref[1]], axis=1)
    cosine, sine = twiddle_ref[0], twiddle_ref[1]
    left = lax.broadcasted_iota(jnp.int32, (1, BLOCK), 1) < N_COL
    place = [lax.rem(to + N_BAND - band, N_BAND) for to in range(N_BAND)]
    waves = WAVES // N_COL

    def load(i, slot):
        flat[slot] = x_ref[:, i].astype(f32).reshape(HALF * ROWS, BLOCK)

    def transform(i, buffer):
        core, level = divmod(i, LEVELS)
        slot = lax.rem(core + half, 2)
        for r in range(0, ROWS, 4):
            twisted = []
            for e in range(r, r + 4, 2):
                pair = [flat[buffer, pl.ds(e + d, HALF, stride=ROWS), :] for d in range(2)]
                x = jnp.concatenate(pair, axis=1).astype(bf16)
                y = jnp.dot(inner, jnp.concatenate([x, x], axis=0), preferred_element_type=f32)
                for d in range(2):
                    lanes = slice(d * BLOCK, (d + 1) * BLOCK)
                    real, imag = y[:N_COL, lanes], y[N_COL:, lanes]
                    twisted.append(jnp.concatenate(
                        [(real * cosine + imag * sine).astype(bf16), (imag * cosine - real * sine).astype(bf16)], axis=1))
            z = jnp.concatenate(twisted, axis=0)
            w = lax.dot_general(outer, z, (((1,), (1,)), ((), ())), preferred_element_type=f32)
            w = w[:2 * waves] + w[2 * waves:]
            for k in range(4 // 2):
                even = w[:waves, k * BLOCK:(k + 1) * BLOCK]
                odd = w[waves:, k * BLOCK:(k + 1) * BLOCK]
                rows = (jnp.where(left, even, pltpu.roll(odd, N_COL, 1)), jnp.where(left, pltpu.roll(even, N_COL, 1), odd))
                for d in range(2):
                    for to in range(N_BAND):
                        out_ref[place[to], slot, level, r + 2 * k + d] = rows[d][to * 8:(to + 1) * 8].astype(bf16)

    load(0, 0)
    for i in range(PAIR):
        if i + 1 < PAIR:
            load(i + 1, (i + 1) % 2)
        transform(i, i % 2)


def fourier(pieces):
    inner, twiddle, outer = tables()
    vmem = pl.BlockSpec(memory_space=pltpu.VMEM)
    return pl.pallas_call(
        fourier_kernel,
        out_shape=jax.ShapeDtypeStruct((N_BAND, 2, LEVELS, ROWS, 8, BLOCK), bf16),
        in_specs=[vmem] * 4,
        out_specs=vmem,
        scratch_shapes=[pltpu.VMEM((2, HALF * ROWS, BLOCK), f32)],
        compiler_params=pltpu.CompilerParams(vmem_limit_bytes=VMEM_BYTES),
        name="fourier",
    )(pieces, jnp.asarray(inner), jnp.asarray(twiddle), jnp.asarray(outer))


def finish_kernel(shifts, *refs):
    count = len(shifts)
    ours, theirs = refs[:count], refs[count:2 * count]
    out_hbm, buffer, sems = refs[-3:]
    band = lax.axis_index("band")
    copies = []
    for k, shift in enumerate(shifts):
        first = lax.rem(band + N_BAND - shift, N_BAND) * ROWS
        for i in range(LEVELS):
            for r in range(ROWS):
                piece = ours[k][0, i, r].astype(f32) + theirs[k][i, r].astype(f32)
                for t in range(4):
                    buffer[k, i, r, :, t * BLOCK:(t + 1) * BLOCK] = piece[2 * t:2 * t + 2]
        copies.append(pltpu.make_async_copy(buffer.at[k], out_hbm.at[:, pl.ds(first, ROWS)], sems.at[k]))
        copies[-1].start()
    for copy in copies:
        copy.wait()


def finish(shifts, ours, theirs, before=None):
    vmem = pl.BlockSpec(memory_space=pltpu.VMEM)
    hbm = pl.BlockSpec(memory_space=pltpu.HBM)
    count = len(shifts)
    rest = [] if before is None else [before]
    return pl.pallas_call(
        functools.partial(finish_kernel, shifts),
        out_shape=jax.ShapeDtypeStruct((LEVELS, N_BAND * ROWS, 2, WAVES // N_BAND), f32),
        in_specs=[vmem] * (2 * count) + [hbm] * len(rest),
        out_specs=hbm,
        scratch_shapes=[
            pltpu.VMEM((count, LEVELS, ROWS, 2, WAVES // N_BAND), f32),
            pltpu.SemaphoreType.DMA((count,)),
        ],
        input_output_aliases={2 * count: 0} if rest else {},
        compiler_params=pltpu.CompilerParams(vmem_limit_bytes=VMEM_BYTES),
        name="finish",
    )(*[ours[shift] for shift in shifts], *[theirs[shift] for shift in shifts], *rest)


def along_z(piece, shift):
    pairs = []
    for band in range(N_BAND):
        for half in range(2):
            for core in range(2):
                to = ((band + shift) % N_BAND * 2 + core) * 2 + half
                pairs.append(((band * 2 + half) * 2 + core, to))
    return lax.ppermute(piece, ("band", "zhi", "core"), pairs)


def shards(fields, inverse, block_costs, row_length):
    updated = relax(fields, inverse, block_costs, row_length)
    half_rows = lax.all_to_all(
        updated.reshape(HALF, PAIR, ROWS, BLOCK), ("core", "y", "x"), split_axis=0, concat_axis=0, tiled=True
    )
    spectra = fourier(half_rows)
    ours = [along_z(spectra[shift], shift) for shift in range(N_BAND)]
    theirs = [lax.ppermute(piece[1], "core", [(0, 1), (1, 0)]) for piece in ours]
    return finish((3,), ours, theirs, finish((0, 1, 2), ours, theirs))


def solution(mesh):
    fine = Mesh(mesh.devices.reshape(N_BAND, 2, 4, 4, 2), ("band",) + COL_AXES)
    return jax.shard_map(
        shards,
        mesh=fine,
        in_specs=(P(None, None, "band", COL_AXES), P(), P(COL_AXES, "band"), P("band")),
        out_specs=P(COL_AXES, None, None, "band"),
        check_vma=False,
    )
```

```python
import functools
import math

import jax
import jax.numpy as jnp
import numpy as np
from jax import lax
from jax.experimental import pallas as pl
from jax.experimental.pallas import tpu as pltpu
from jax.sharding import Mesh, PartitionSpec as P

f32 = jnp.float32
bf16 = jnp.bfloat16
VMEM_BYTES = 40 * 1024 * 1024
RELAX_BYTES = 61 * 1024 * 1024

FIELDS = 4
LEV = 80
CMAX = 8
ROWS = 8
BLOCK = 128
N_COL = 64
N_BAND = 4
NLON = N_COL * BLOCK
WAVES = 2048
LEVELS = FIELDS * LEV // N_COL
COL_AXES = ("zhi", "y", "x", "core")
HALF = N_COL // 2
PAIRS = N_COL // 4
PAIR = 2 * LEVELS


def split_bf16(table):
    high = table.astype(np.float32).astype(jnp.bfloat16)
    low = (table - high.astype(np.float64)).astype(np.float32).astype(jnp.bfloat16)
    return high, low


def tables():
    q = np.arange(N_COL)
    s = np.arange(HALF)
    angle = 2.0 * np.pi / N_COL * ((q[:, None] * s[None, :]) % N_COL)
    inner = np.concatenate([np.cos(angle), -np.sin(angle)], axis=0)
    sign = np.where(np.arange(2 * N_COL) % 2 == 0, 1.0, -1.0)
    inner = np.stack([inner, inner * sign[:, None]])
    inner = np.concatenate(split_bf16(inner), axis=2)
    b = np.arange(BLOCK)
    angle = 2.0 * np.pi / NLON * (q[:, None] * b[None, :])
    twiddle = np.stack([np.cos(angle), np.sin(angle)]).astype(np.float32)
    p = np.arange(WAVES // N_COL).reshape(-1, 2).T.reshape(-1)
    angle = 2.0 * np.pi / BLOCK * ((p[:, None] * b[None, :]) % BLOCK)
    cosine, sine = np.cos(angle), np.sin(angle)
    real_row = np.concatenate([cosine, sine], axis=1)
    imag_row = np.concatenate([-sine, cosine], axis=1)
    outer = np.stack([real_row, imag_row], axis=1).reshape(2 * WAVES // N_COL, 2 * BLOCK) / math.sqrt(NLON)
    outer = np.concatenate(split_bf16(outer), axis=0)
    outer = np.stack([outer[:, :BLOCK], outer[:, BLOCK:]])
    return inner, twiddle, outer


def relax_kernel(
    cost_hbm, length_hbm, fields_hbm, inverse_hbm, out_hbm,
    cost_ref, length_ref, fields_ref, inverse_ref, flat, state, start, out_ref, sems, out_sems,
):
    copies = [pltpu.make_async_copy(fields_hbm.at[f], fields_ref.at[f], sems.at[f]) for f in range(FIELDS)]
    small = [
        pltpu.make_async_copy(inverse_hbm, inverse_ref, sems.at[FIELDS]),
        pltpu.make_async_copy(cost_hbm, cost_ref, sems.at[FIELDS + 1]),
        pltpu.make_async_copy(length_hbm, length_ref, sems.at[FIELDS + 2]),
    ]
    for copy in small + copies:
        copy.start()
    first = lax.axis_index(COL_AXES) * BLOCK
    for f in range(FIELDS):
        copies[f].wait()
        flat[f * LEV * ROWS:(f + 1) * LEV * ROWS, :] = fields_ref[f].astype(f32).reshape(LEV * ROWS, BLOCK)
        for r in range(ROWS):
            piece = flat[pl.ds(f * LEV * ROWS + r, LEV, stride=ROWS), :].astype(bf16)
            state[f, :, r * BLOCK:(r + 1) * BLOCK] = piece
            start[f, :, r * BLOCK:(r + 1) * BLOCK] = piece
    for copy in small:
        copy.wait()
    costs = [cost_ref[0, r] for r in range(ROWS)]
    most = costs[0]
    for r in range(1, ROWS):
        most = jnp.maximum(most, costs[r])
    cost_lanes = jnp.concatenate([jnp.full((16, BLOCK), costs[r], jnp.int32) for r in range(ROWS)], axis=1).astype(f32).astype(bf16)

    def sweep(s):
        step = jnp.full((16, ROWS * BLOCK), s, jnp.int32).astype(f32).astype(bf16)
        for f in range(FIELDS):
            for t in range(0, ROWS * BLOCK, 2 * BLOCK):
                active = jnp.concatenate([cost_lanes[:, t:t + 2 * BLOCK] > step[:, t:t + 2 * BLOCK]] * (LEV // 16), axis=0)
                now = state[f, :, t:t + 2 * BLOCK]
                new = jnp.dot(inverse_ref[f], now, preferred_element_type=f32)
                state[f, :, t:t + 2 * BLOCK] = jnp.where(active, new.astype(bf16), now)

    sweep(0)

    @pl.when(most > 1)
    def _():
        for s in range(1, CMAX):
            sweep(s)

    lane = first + lax.broadcasted_iota(jnp.int32, (1, BLOCK), 1)
    keep = [lane < length_ref[r] for r in range(ROWS)]
    sends = []
    for f in range(FIELDS):
        for r in range(ROWS):
            lanes = slice(r * BLOCK, (r + 1) * BLOCK)
            initial = start[f, :, lanes].astype(f32)
            relaxed = state[f, :, lanes].astype(f32)
            tendency = (relaxed - initial).astype(bf16).astype(f32)
            updated = (initial + tendency).astype(bf16).astype(f32)
            flat[pl.ds(f * LEV * ROWS + r, LEV, stride=ROWS), :] = jnp.where(keep[r], updated, 0.0)
        piece = flat[f * LEV * ROWS:(f + 1) * LEV * ROWS, :].reshape(LEV // PAIR, PAIR, ROWS, BLOCK)
        out_ref[f] = piece.astype(bf16)
        first = f % 2 * (LEV // PAIR)
        sends.append(pltpu.make_async_copy(out_ref.at[f], out_hbm.at[pl.ds(first, LEV // PAIR), f // 2], out_sems.at[f]))
        sends[-1].start()
    for send in sends:
        send.wait()


def relax(fields, inverse, costs, lengths):
    return pl.pallas_call(
        relax_kernel,
        out_shape=jax.ShapeDtypeStruct((PAIRS, 2, PAIR, ROWS, BLOCK), bf16),
        in_specs=[pl.BlockSpec(memory_space=pltpu.HBM)] * 4,
        out_specs=pl.BlockSpec(memory_space=pltpu.HBM),
        scratch_shapes=[
            pltpu.SMEM((1, ROWS), jnp.int32),
            pltpu.SMEM((ROWS,), jnp.int32),
            pltpu.VMEM((FIELDS, LEV, ROWS, BLOCK), bf16),
            pltpu.VMEM((FIELDS, LEV, LEV), bf16),
            pltpu.VMEM((FIELDS * LEV * ROWS, BLOCK), f32),
            pltpu.VMEM((FIELDS, LEV, ROWS * BLOCK), bf16),
            pltpu.VMEM((FIELDS, LEV, ROWS * BLOCK), bf16),
            pltpu.VMEM((FIELDS, LEV // PAIR, PAIR, ROWS, BLOCK), bf16),
            pltpu.SemaphoreType.DMA((FIELDS + 3,)),
            pltpu.SemaphoreType.DMA((FIELDS,)),
        ],
        compiler_params=pltpu.CompilerParams(vmem_limit_bytes=RELAX_BYTES),
        name="relax",
    )(costs, lengths, fields, inverse)


def fourier_kernel(x_ref, inner_ref, twiddle_ref, outer_ref, out_ref, flat):
    half = lax.axis_index("zhi")
    band = lax.axis_index("band")
    inner = inner_ref[half]
    outer = jnp.concatenate([outer_ref[0], outer_ref[1]], axis=1)
    cosine, sine = twiddle_ref[0], twiddle_ref[1]
    left = lax.broadcasted_iota(jnp.int32, (1, BLOCK), 1) < N_COL
    place = [lax.rem(to + N_BAND - band, N_BAND) for to in range(N_BAND)]
    waves = WAVES // N_COL

    def load(i, slot):
        flat[slot] = x_ref[:, i].astype(f32).reshape(HALF * ROWS, BLOCK)

    def transform(i, buffer):
        core, level = divmod(i, LEVELS)
        slot = lax.rem(core + half, 2)
        for r in range(0, ROWS, 4):
            twisted = []
            for e in range(r, r + 4, 2):
                pair = [flat[buffer, pl.ds(e + d, HALF, stride=ROWS), :] for d in range(2)]
                x = jnp.concatenate(pair, axis=1).astype(bf16)
                y = jnp.dot(inner, jnp.concatenate([x, x], axis=0), preferred_element_type=f32)
                for d in range(2):
                    lanes = slice(d * BLOCK, (d + 1) * BLOCK)
                    real, imag = y[:N_COL, lanes], y[N_COL:, lanes]
                    twisted.append(jnp.concatenate(
                        [(real * cosine + imag * sine).astype(bf16), (imag * cosine - real * sine).astype(bf16)], axis=1))
            z = jnp.concatenate(twisted, axis=0)
            w = lax.dot_general(outer, z, (((1,), (1,)), ((), ())), preferred_element_type=f32)
            w = w[:2 * waves] + w[2 * waves:]
            for k in range(4 // 2):
                even = w[:waves, k * BLOCK:(k + 1) * BLOCK]
                odd = w[waves:, k * BLOCK:(k + 1) * BLOCK]
                rows = (jnp.where(left, even, pltpu.roll(odd, N_COL, 1)), jnp.where(left, pltpu.roll(even, N_COL, 1), odd))
                for d in range(2):
                    for to in range(N_BAND):
                        out_ref[place[to], slot, level, r + 2 * k + d] = rows[d][to * 8:(to + 1) * 8].astype(bf16)

    load(0, 0)
    for i in range(PAIR):
        if i + 1 < PAIR:
            load(i + 1, (i + 1) % 2)
        transform(i, i % 2)


def fourier(pieces):
    inner, twiddle, outer = tables()
    vmem = pl.BlockSpec(memory_space=pltpu.VMEM)
    return pl.pallas_call(
        fourier_kernel,
        out_shape=jax.ShapeDtypeStruct((N_BAND, 2, LEVELS, ROWS, 8, BLOCK), bf16),
        in_specs=[vmem] * 4,
        out_specs=vmem,
        scratch_shapes=[pltpu.VMEM((2, HALF * ROWS, BLOCK), f32)],
        compiler_params=pltpu.CompilerParams(vmem_limit_bytes=VMEM_BYTES),
        name="fourier",
    )(pieces, jnp.asarray(inner), jnp.asarray(twiddle), jnp.asarray(outer))


def finish_kernel(shifts, *refs):
    count = len(shifts)
    ours, theirs = refs[:count], refs[count:2 * count]
    out_hbm, buffer, sems = refs[-3:]
    band = lax.axis_index("band")
    copies = []
    for k, shift in enumerate(shifts):
        first = lax.rem(band + N_BAND - shift, N_BAND) * ROWS
        for i in range(LEVELS):
            for r in range(ROWS):
                piece = ours[k][0, i, r].astype(f32) + theirs[k][i, r].astype(f32)
                for t in range(4):
                    buffer[k, i, r, :, t * BLOCK:(t + 1) * BLOCK] = piece[2 * t:2 * t + 2]
        copies.append(pltpu.make_async_copy(buffer.at[k], out_hbm.at[:, pl.ds(first, ROWS)], sems.at[k]))
        copies[-1].start()
    for copy in copies:
        copy.wait()


def finish(shifts, ours, theirs, before=None):
    vmem = pl.BlockSpec(memory_space=pltpu.VMEM)
    hbm = pl.BlockSpec(memory_space=pltpu.HBM)
    count = len(shifts)
    rest = [] if before is None else [before]
    return pl.pallas_call(
        functools.partial(finish_kernel, shifts),
        out_shape=jax.ShapeDtypeStruct((LEVELS, N_BAND * ROWS, 2, WAVES // N_BAND), f32),
        in_specs=[vmem] * (2 * count) + [hbm] * len(rest),
        out_specs=hbm,
        scratch_shapes=[
            pltpu.VMEM((count, LEVELS, ROWS, 2, WAVES // N_BAND), f32),
            pltpu.SemaphoreType.DMA((count,)),
        ],
        input_output_aliases={2 * count: 0} if rest else {},
        compiler_params=pltpu.CompilerParams(vmem_limit_bytes=VMEM_BYTES),
        name="finish",
    )(*[ours[shift] for shift in shifts], *[theirs[shift] for shift in shifts], *rest)


def along_z(piece, shift):
    pairs = []
    for band in range(N_BAND):
        for half in range(2):
            for core in range(2):
                to = ((band + shift) % N_BAND * 2 + core) * 2 + half
                pairs.append(((band * 2 + half) * 2 + core, to))
    return lax.ppermute(piece, ("band", "zhi", "core"), pairs)


def shards(fields, inverse, block_costs, row_length):
    updated = relax(fields, inverse, block_costs, row_length)
    half_rows = lax.all_to_all(
        updated.reshape(HALF, PAIR, ROWS, BLOCK), ("y", "x", "core"), split_axis=0, concat_axis=0, tiled=True
    )
    spectra = fourier(half_rows)
    ours = [along_z(spectra[shift], shift) for shift in range(N_BAND)]
    theirs = [lax.ppermute(piece[1], "core", [(0, 1), (1, 0)]) for piece in ours]
    return finish((3,), ours, theirs, finish((0, 1, 2), ours, theirs))


def solution(mesh):
    fine = Mesh(mesh.devices.reshape(N_BAND, 2, 4, 4, 2), ("band",) + COL_AXES)
    return jax.shard_map(
        shards,
        mesh=fine,
        in_specs=(P(None, None, "band", COL_AXES), P(), P(COL_AXES, "band"), P("band")),
        out_specs=P(COL_AXES, None, None, "band"),
        check_vma=False,
    )
```

```python
import functools
import math

import jax
import jax.numpy as jnp
import numpy as np
from jax import lax
from jax.experimental import pallas as pl
from jax.experimental.pallas import tpu as pltpu
from jax.sharding import Mesh, PartitionSpec as P

f32 = jnp.float32
bf16 = jnp.bfloat16
VMEM_BYTES = 40 * 1024 * 1024
RELAX_BYTES = 61 * 1024 * 1024

FIELDS = 4
LEV = 80
CMAX = 8
ROWS = 8
BLOCK = 128
N_COL = 64
N_BAND = 4
NLON = N_COL * BLOCK
WAVES = 2048
LEVELS = FIELDS * LEV // N_COL
COL_AXES = ("zhi", "y", "x", "core")
HALF = N_COL // 2
PAIRS = N_COL // 4
PAIR = 2 * LEVELS


def split_bf16(table):
    high = table.astype(np.float32).astype(jnp.bfloat16)
    low = (table - high.astype(np.float64)).astype(np.float32).astype(jnp.bfloat16)
    return high, low


def tables():
    q = np.arange(N_COL)
    s = np.arange(HALF)
    angle = 2.0 * np.pi / N_COL * ((q[:, None] * s[None, :]) % N_COL)
    inner = np.concatenate([np.cos(angle), -np.sin(angle)], axis=0)
    sign = np.where(np.arange(2 * N_COL) % 2 == 0, 1.0, -1.0)
    inner = np.stack([inner, inner * sign[:, None]])
    inner = np.concatenate(split_bf16(inner), axis=2)
    b = np.arange(BLOCK)
    angle = 2.0 * np.pi / NLON * (q[:, None] * b[None, :])
    twiddle = np.stack([np.cos(angle), np.sin(angle)]).astype(np.float32)
    p = np.arange(WAVES // N_COL).reshape(-1, 2).T.reshape(-1)
    angle = 2.0 * np.pi / BLOCK * ((p[:, None] * b[None, :]) % BLOCK)
    cosine, sine = np.cos(angle), np.sin(angle)
    real_row = np.concatenate([cosine, sine], axis=1)
    imag_row = np.concatenate([-sine, cosine], axis=1)
    outer = np.stack([real_row, imag_row], axis=1).reshape(2 * WAVES // N_COL, 2 * BLOCK) / math.sqrt(NLON)
    outer = np.concatenate(split_bf16(outer), axis=0)
    outer = np.stack([outer[:, :BLOCK], outer[:, BLOCK:]])
    return inner, twiddle, outer


def relax_kernel(
    cost_hbm, length_hbm, fields_hbm, inverse_hbm, out_hbm,
    cost_ref, length_ref, fields_ref, inverse_ref, flat, state, start, out_ref, sems, out_sems,
):
    copies = [pltpu.make_async_copy(fields_hbm.at[f], fields_ref.at[f], sems.at[f]) for f in range(FIELDS)]
    small = [
        pltpu.make_async_copy(inverse_hbm, inverse_ref, sems.at[FIELDS]),
        pltpu.make_async_copy(cost_hbm, cost_ref, sems.at[FIELDS + 1]),
        pltpu.make_async_copy(length_hbm, length_ref, sems.at[FIELDS + 2]),
    ]
    for copy in copies + small:
        copy.start()
    first = lax.axis_index(COL_AXES) * BLOCK
    for f in range(FIELDS):
        copies[f].wait()
        flat[f * LEV * ROWS:(f + 1) * LEV * ROWS, :] = fields_ref[f].astype(f32).reshape(LEV * ROWS, BLOCK)
        for r in range(ROWS):
            piece = flat[pl.ds(f * LEV * ROWS + r, LEV, stride=ROWS), :].astype(bf16)
            state[f, :, r * BLOCK:(r + 1) * BLOCK] = piece
            start[f, :, r * BLOCK:(r + 1) * BLOCK] = piece
    for copy in small:
        copy.wait()
    costs = [cost_ref[0, r] for r in range(ROWS)]
    most = costs[0]
    for r in range(1, ROWS):
        most = jnp.maximum(most, costs[r])
    cost_lanes = jnp.concatenate([jnp.full((16, BLOCK), costs[r], jnp.int32) for r in range(ROWS)], axis=1).astype(f32).astype(bf16)

    def sweep(s):
        step = jnp.full((16, ROWS * BLOCK), s, jnp.int32).astype(f32).astype(bf16)
        for f in range(FIELDS):
            for t in range(0, ROWS * BLOCK, 2 * BLOCK):
                active = jnp.concatenate([cost_lanes[:, t:t + 2 * BLOCK] > step[:, t:t + 2 * BLOCK]] * (LEV // 16), axis=0)
                now = state[f, :, t:t + 2 * BLOCK]
                new = jnp.dot(inverse_ref[f], now, preferred_element_type=f32)
                state[f, :, t:t + 2 * BLOCK] = jnp.where(active, new.astype(bf16), now)

    sweep(0)

    @pl.when(most > 1)
    def _():
        for s in range(1, CMAX):
            sweep(s)

    lane = first + lax.broadcasted_iota(jnp.int32, (1, BLOCK), 1)
    keep = [lane < length_ref[r] for r in range(ROWS)]
    sends = []
    for f in range(FIELDS):
        for r in range(ROWS):
            lanes = slice(r * BLOCK, (r + 1) * BLOCK)
            initial = start[f, :, lanes].astype(f32)
            relaxed = state[f, :, lanes].astype(f32)
            tendency = (relaxed - initial).astype(bf16).astype(f32)
            updated = (initial + tendency).astype(bf16).astype(f32)
            flat[pl.ds(f * LEV * ROWS + r, LEV, stride=ROWS), :] = jnp.where(keep[r], updated, 0.0)
        piece = flat[f * LEV * ROWS:(f + 1) * LEV * ROWS, :].reshape(LEV // PAIR, PAIR, ROWS, BLOCK)
        out_ref[f] = piece.astype(bf16)
        first = f % 2 * (LEV // PAIR)
        sends.append(pltpu.make_async_copy(out_ref.at[f], out_hbm.at[pl.ds(first, LEV // PAIR), f // 2], out_sems.at[f]))
        sends[-1].start()
    for send in sends:
        send.wait()


def relax(fields, inverse, costs, lengths):
    return pl.pallas_call(
        relax_kernel,
        out_shape=jax.ShapeDtypeStruct((PAIRS, 2, PAIR, ROWS, BLOCK), bf16),
        in_specs=[pl.BlockSpec(memory_space=pltpu.HBM)] * 4,
        out_specs=pl.BlockSpec(memory_space=pltpu.HBM),
        scratch_shapes=[
            pltpu.SMEM((1, ROWS), jnp.int32),
            pltpu.SMEM((ROWS,), jnp.int32),
            pltpu.VMEM((FIELDS, LEV, ROWS, BLOCK), bf16),
            pltpu.VMEM((FIELDS, LEV, LEV), bf16),
            pltpu.VMEM((FIELDS * LEV * ROWS, BLOCK), f32),
            pltpu.VMEM((FIELDS, LEV, ROWS * BLOCK), bf16),
            pltpu.VMEM((FIELDS, LEV, ROWS * BLOCK), bf16),
            pltpu.VMEM((FIELDS, LEV // PAIR, PAIR, ROWS, BLOCK), bf16),
            pltpu.SemaphoreType.DMA((FIELDS + 3,)),
            pltpu.SemaphoreType.DMA((FIELDS,)),
        ],
        compiler_params=pltpu.CompilerParams(vmem_limit_bytes=RELAX_BYTES),
        name="relax",
    )(costs, lengths, fields, inverse)


def fourier_kernel(x_ref, inner_ref, twiddle_ref, outer_ref, out_ref, flat):
    half = lax.axis_index("zhi")
    band = lax.axis_index("band")
    inner = inner_ref[half]
    outer = jnp.concatenate([outer_ref[0], outer_ref[1]], axis=1)
    cosine, sine = twiddle_ref[0], twiddle_ref[1]
    left = lax.broadcasted_iota(jnp.int32, (1, BLOCK), 1) < N_COL
    place = [lax.rem(to + N_BAND - band, N_BAND) for to in range(N_BAND)]
    waves = WAVES // N_COL

    def load(i, slot):
        flat[slot] = x_ref[:, i].astype(f32).reshape(HALF * ROWS, BLOCK)

    def transform(i, buffer):
        core, level = divmod(i, LEVELS)
        slot = lax.rem(core + half, 2)
        for r in range(0, ROWS, 2):
            twisted = []
            for e in range(r, r + 2, 2):
                pair = [flat[buffer, pl.ds(e + d, HALF, stride=ROWS), :] for d in range(2)]
                x = jnp.concatenate(pair, axis=1).astype(bf16)
                y = jnp.dot(inner, jnp.concatenate([x, x], axis=0), preferred_element_type=f32)
                for d in range(2):
                    lanes = slice(d * BLOCK, (d + 1) * BLOCK)
                    real, imag = y[:N_COL, lanes], y[N_COL:, lanes]
                    twisted.append(jnp.concatenate(
                        [(real * cosine + imag * sine).astype(bf16), (imag * cosine - real * sine).astype(bf16)], axis=1))
            z = jnp.concatenate(twisted, axis=0)
            w = lax.dot_general(outer, z, (((1,), (1,)), ((), ())), preferred_element_type=f32)
            w = w[:2 * waves] + w[2 * waves:]
            for k in range(1):
                even = w[:waves, k * BLOCK:(k + 1) * BLOCK]
                odd = w[waves:, k * BLOCK:(k + 1) * BLOCK]
                rows = (jnp.where(left, even, pltpu.roll(odd, N_COL, 1)), jnp.where(left, pltpu.roll(even, N_COL, 1), odd))
                for d in range(2):
                    for to in range(N_BAND):
                        out_ref[place[to], slot, level, r + 2 * k + d] = rows[d][to * 8:(to + 1) * 8].astype(bf16)

    load(0, 0)
    for i in range(PAIR):
        if i + 1 < PAIR:
            load(i + 1, (i + 1) % 2)
        transform(i, i % 2)


def fourier(pieces):
    inner, twiddle, outer = tables()
    vmem = pl.BlockSpec(memory_space=pltpu.VMEM)
    return pl.pallas_call(
        fourier_kernel,
        out_shape=jax.ShapeDtypeStruct((N_BAND, 2, LEVELS, ROWS, 8, BLOCK), bf16),
        in_specs=[vmem] * 4,
        out_specs=vmem,
        scratch_shapes=[pltpu.VMEM((2, HALF * ROWS, BLOCK), f32)],
        compiler_params=pltpu.CompilerParams(vmem_limit_bytes=VMEM_BYTES),
        name="fourier",
    )(pieces, jnp.asarray(inner), jnp.asarray(twiddle), jnp.asarray(outer))


def finish_kernel(shifts, *refs):
    count = len(shifts)
    ours, theirs = refs[:count], refs[count:2 * count]
    out_hbm, buffer, sems = refs[-3:]
    band = lax.axis_index("band")
    copies = []
    for k, shift in enumerate(shifts):
        first = lax.rem(band + N_BAND - shift, N_BAND) * ROWS
        for i in range(LEVELS):
            for r in range(ROWS):
                piece = ours[k][0, i, r].astype(f32) + theirs[k][i, r].astype(f32)
                for t in range(4):
                    buffer[k, i, r, :, t * BLOCK:(t + 1) * BLOCK] = piece[2 * t:2 * t + 2]
        copies.append(pltpu.make_async_copy(buffer.at[k], out_hbm.at[:, pl.ds(first, ROWS)], sems.at[k]))
        copies[-1].start()
    for copy in copies:
        copy.wait()


def finish(shifts, ours, theirs, before=None):
    vmem = pl.BlockSpec(memory_space=pltpu.VMEM)
    hbm = pl.BlockSpec(memory_space=pltpu.HBM)
    count = len(shifts)
    rest = [] if before is None else [before]
    return pl.pallas_call(
        functools.partial(finish_kernel, shifts),
        out_shape=jax.ShapeDtypeStruct((LEVELS, N_BAND * ROWS, 2, WAVES // N_BAND), f32),
        in_specs=[vmem] * (2 * count) + [hbm] * len(rest),
        out_specs=hbm,
        scratch_shapes=[
            pltpu.VMEM((count, LEVELS, ROWS, 2, WAVES // N_BAND), f32),
            pltpu.SemaphoreType.DMA((count,)),
        ],
        input_output_aliases={2 * count: 0} if rest else {},
        compiler_params=pltpu.CompilerParams(vmem_limit_bytes=VMEM_BYTES),
        name="finish",
    )(*[ours[shift] for shift in shifts], *[theirs[shift] for shift in shifts], *rest)


def along_z(piece, shift):
    pairs = []
    for band in range(N_BAND):
        for half in range(2):
            for core in range(2):
                to = ((band + shift) % N_BAND * 2 + core) * 2 + half
                pairs.append(((band * 2 + half) * 2 + core, to))
    return lax.ppermute(piece, ("band", "zhi", "core"), pairs)


def shards(fields, inverse, block_costs, row_length):
    updated = relax(fields, inverse, block_costs, row_length)
    half_rows = lax.all_to_all(
        updated.reshape(HALF, PAIR, ROWS, BLOCK), ("y", "x", "core"), split_axis=0, concat_axis=0, tiled=True
    )
    spectra = fourier(half_rows)
    ours = [along_z(spectra[shift], shift) for shift in range(N_BAND)]
    theirs = [lax.ppermute(piece[1], "core", [(0, 1), (1, 0)]) for piece in ours]
    return finish((3,), ours, theirs, finish((0, 1, 2), ours, theirs))


def solution(mesh):
    fine = Mesh(mesh.devices.reshape(N_BAND, 2, 4, 4, 2), ("band",) + COL_AXES)
    return jax.shard_map(
        shards,
        mesh=fine,
        in_specs=(P(None, None, "band", COL_AXES), P(), P(COL_AXES, "band"), P("band")),
        out_specs=P(COL_AXES, None, None, "band"),
        check_vma=False,
    )
```
